32 devices in a mesh: chan: 4 (over x, core), blk: 8 (over z, y).
Axes of the slice: x: 2, y: 2, z: 4, core: 2. Of those that a mesh axis runs over, the one named last changes fastest.
Arguments:
- voltages: bfloat16 [64, 262144], P('blk', 'chan'), may hold values from -6 to 6
- fir_taps: float32 [8, 4096], replicated, may hold values from -2.1 to 2.1
Outputs:
- visibilities: float32 [2, 64, 64, 2048], P(None, 'blk', None, 'chan')
The draws below stay inside these ranges and needn't reach their ends.
All inputs are finite; a program needn't handle non-finite values.
Results may differ from the reference program's by a relative error of at most 0.0036.
Values may be sent and summed in bfloat16 or wider, within the bound.
A program may use at most 192 MiB of HBM per device.

```python
import math
import jax
import jax.numpy as jnp
from jax import lax

TAPS = 8
L = 4096
C = 2048
FEEDS = 64
S = 64


def level_of(key, shape, shards, low, largest):
    gain, own = 1.0, jax.random.fold_in(key, 6)
    for dim, parts in shards:
        draws = jnp.exp(jax.random.uniform(jax.random.fold_in(own, dim), (parts,), jnp.float32, low / len(shards), largest / len(shards)))
        gain = gain * jnp.repeat(draws, shape[dim] // parts).reshape([-1 if axis == dim else 1 for axis in range(len(shape))])
    return gain


def noise(own_key, shape, deviation, most, shards=(), kind=jnp.bfloat16):
    array = deviation * jax.random.normal(own_key, shape, jnp.float32)
    if shards:
        array = array * level_of(own_key, shape, shards, -0.22, 0.18)
    return jnp.clip(array, -most, most).astype(kind)


def setup_inputs(seed: int = 0) -> dict:
    streams_of = jax.random.split(jax.random.key(seed), 3)
    return {
        "voltages": noise(streams_of[0], (FEEDS, S * L), 1.0, 6.0, ((0, 8), (1, 4))),
        "fir_taps": noise(streams_of[1], (TAPS, L), 0.35, 2.1, (), jnp.float32),
    }


def dft_table(first_channel, channel_count, length):
    channel_ids = first_channel + jnp.arange(channel_count, dtype=jnp.int32)
    sample_ids = jnp.arange(length, dtype=jnp.int32)
    phase_index = sample_ids[:, None] * channel_ids[None, :] % length
    angles = phase_index.astype(jnp.float32) * (2.0 * math.pi / length)
    normaliser = 1.0 / math.sqrt(length)
    return jnp.concatenate([jnp.cos(angles) * normaliser, -jnp.sin(angles) * normaliser], axis=1)

def reference(voltages, fir_taps):
    feed_count = voltages.shape[0]
    own_frames = voltages.reshape(feed_count, S, L)
    zero_frames = jnp.zeros((feed_count, TAPS - 1, L), voltages.dtype)
    extended = jnp.concatenate([zero_frames, own_frames], axis=1)
    filtered = jnp.zeros((feed_count, S, L), jnp.float32)
    for tap_index in range(TAPS):
        filtered = filtered + fir_taps[tap_index][None, None, :] * extended[:, tap_index:tap_index + S, :].astype(jnp.float32)
    frame_rows = filtered.reshape(feed_count * S, L)
    block_width = min(C, 512)
    pieces = []
    for first_channel in range(0, C, block_width):
        cos_sin_table = dft_table(first_channel, block_width, L)
        product = jnp.dot(frame_rows, cos_sin_table, precision=lax.Precision.HIGHEST, preferred_element_type=jnp.float32)
        pieces.append(product.reshape(feed_count * S, 2, block_width))
    spectra = jnp.concatenate(pieces, axis=2).astype(jnp.bfloat16).reshape(feed_count, S, 2, C)
    values = spectra.astype(jnp.float32)
    inverse_count = 1.0 / S
    results = []
    for first_channel in range(0, C, block_width):
        part = values[:, :, :, first_channel:first_channel + block_width]
        gram_terms = jnp.einsum('itpc,jtqc->ipjqc', part, part)
        real_part = gram_terms[:, 0, :, 0] + gram_terms[:, 1, :, 1]
        imag_part = gram_terms[:, 1, :, 0] - gram_terms[:, 0, :, 1]
        results.append(jnp.stack([real_part, imag_part]) * inverse_count)
    return jnp.concatenate(results, axis=3)
```

```python
import functools
import math

import jax
import jax.numpy as jnp
import numpy as np
from jax import lax
from jax.experimental import pallas as pl
from jax.experimental.pallas import tpu as pltpu
from jax.sharding import PartitionSpec as P

TAPS = 8
L = 4096
C = 2048
N2 = 128
N1 = L // N2
HALF = C // N1
VMEM = 56 * 1024 * 1024


def tables():
    n2 = np.arange(N2)
    angle = 2.0 * np.pi * (np.arange(N1)[:, None] * n2[None, :] % L) / L
    twiddle = np.stack([np.cos(angle), np.sin(angle)]).astype(np.float32)
    angle = 2.0 * np.pi * (np.arange(HALF)[:, None] * n2[None, :] % N2) / N2
    cos, sin = np.cos(angle) / math.sqrt(L), np.sin(angle) / math.sqrt(L)
    matrix = np.block([[cos, sin], [-sin, cos]])
    high = matrix.astype(jnp.bfloat16)
    low = (matrix - high.astype(np.float64)).astype(jnp.bfloat16)
    return twiddle, high, low


def times(scale, value):
    return None if value is None else scale * value


def plus(a, b):
    return b if a is None else a if b is None else a + b


def minus(a, b):
    return a if b is None else -b if a is None else a - b


def real_dft(values):
    n = len(values)
    if n == 1:
        return [(values[0], None)]
    half = n // 2
    even, odd = real_dft(values[0::2]), real_dft(values[1::2])
    result = [None] * (half + 1)
    for k in range(half // 2 + 1):
        (er, ei), (odr, odi) = even[k], odd[k]
        if k == 0:
            tr, ti = odr, odi
        elif 4 * k == n:
            tr, ti = odi, -odr
        else:
            c, s = math.cos(2 * math.pi * k / n), math.sin(2 * math.pi * k / n)
            tr = plus(times(c, odr), times(s, odi))
            ti = minus(times(c, odi), times(s, odr))
        result[half - k] = (minus(er, tr), minus(ti, ei))
        result[k] = (plus(er, tr), plus(ei, ti))
    return result


def fir_stage(volt, halo, taps, filtered, frames):
    @pl.loop(0, N1)
    def _(n1):
        lane = pl.multiple_of(n1 * N2, N2)
        weights = [jnp.broadcast_to(taps[t : t + 1, pl.ds(lane, N2)], (8, N2)) for t in range(TAPS)]
        window = [halo[:, pl.ds(f * L + lane, N2)].astype(jnp.float32) for f in range(TAPS - 1)]
        for f in range(frames):
            window.append(volt[:, pl.ds(f * L + lane, N2)].astype(jnp.float32))
            total = weights[0] * window[f]
            for t in range(1, TAPS):
                total = total + weights[t] * window[f + t]
            filtered[f * N1 + n1] = total


def first_stage(filtered, twiddle, turned, frames):
    @pl.loop(0, frames)
    def _(f):
        spectrum = real_dft([filtered[f * N1 + n1] for n1 in range(N1)])
        row = pl.multiple_of(f * 8, 8)
        for k1 in range(N1):
            if 2 * k1 <= N1:
                zr, zi = spectrum[k1]
            else:
                zr, zi = spectrum[N1 - k1]
                zi = -zi
            c = twiddle[0, k1 : k1 + 1, :]
            s = twiddle[1, k1 : k1 + 1, :]
            if k1 == 0:
                re, im = zr, jnp.zeros_like(zr)
            elif zi is None:
                re, im = c * zr, -(s * zr)
            else:
                re, im = c * zr + s * zi, c * zi - s * zr
            turned[k1, pl.ds(row, 8), pl.ds(0, N2)] = re
            turned[k1, pl.ds(row, 8), pl.ds(N2, N2)] = im


def second_stage(turned, high, low, ordered):
    contract = (((1,), (1,)), ((), ()))
    wh, wl = high[...], low[...]
    for k1 in range(N1):
        z = turned[k1]
        zh = z.astype(jnp.bfloat16)
        zl = (z - zh.astype(jnp.float32)).astype(jnp.bfloat16)
        out = lax.dot_general(wl, zh, contract, preferred_element_type=jnp.float32)
        out = out + lax.dot_general(wh, zl, contract, preferred_element_type=jnp.float32)
        out = out + lax.dot_general(wh, zh, contract, preferred_element_type=jnp.float32)
        for p in range(2):
            ordered[pl.ds(p * C + k1, HALF, stride=N1), :] = out[p * HALF : (p + 1) * HALF]


def spectra_kernel(frames, parts, volt, halo, taps, twiddle, high, low, out, filtered, turned, ordered):
    fir_stage(volt, halo, taps, filtered, frames)
    first_stage(filtered, twiddle, turned, frames)
    second_stage(turned, high, low, ordered)
    chn = C // parts

    @pl.loop(0, parts)
    def _(d):
        for p in range(2):
            out[d, p] = ordered[pl.ds(pl.multiple_of(p * C + d * chn, chn), chn), :].astype(jnp.bfloat16)


def regroup(groups, lane):
    count = len(groups)
    d = 1
    while d < count:
        low_side = (lane & d) == 0
        result = list(groups)
        for g in range(count):
            if g & d == 0:
                a, b = groups[g], groups[g | d]
                result[g] = jnp.where(low_side, a, pltpu.roll(b, d, 1))
                result[g | d] = jnp.where(low_side, pltpu.roll(a, 128 - d, 1), b)
        groups = result
        d *= 2
    return groups


def gather_feeds(get, blk, chan, chn, grouped):
    lane = lax.broadcasted_iota(jnp.int32, (chn, 128), 1)

    @pl.loop(0, blk)
    def _(b):
        arrays = [get(c, b, p).astype(jnp.float32) for p in range(2) for c in range(chan)]
        for feed, value in enumerate(regroup(arrays, lane)):
            row = pl.multiple_of((b * 8 + feed) * chn, chn)
            grouped[pl.ds(row, chn), :] = value


def correlate(grouped, blk, chan, chn, spectra_count, put):
    feeds = blk * 8
    lane = lax.broadcasted_iota(jnp.int32, (feeds, 128), 1)
    real_lane = (lane & chan) == 0
    contract = (((1,), (1,)), ((), ()))

    def one(ch):
        value = grouped[pl.ds(ch, feeds, stride=chn), :]
        other = jnp.where(real_lane, -pltpu.roll(value, 128 - chan, 1), pltpu.roll(value, chan, 1))
        left = value.astype(jnp.bfloat16)
        right = jnp.concatenate([left, other.astype(jnp.bfloat16)], axis=0)
        out = lax.dot_general(left, right, contract, preferred_element_type=jnp.float32)
        return out * (1.0 / spectra_count)

    @pl.loop(0, chn // 2)
    def _(h):
        first, second = one(2 * h), one(2 * h + 1)
        for b in range(blk):
            rows = jnp.concatenate([first[b * 8 : b * 8 + 8], second[b * 8 : b * 8 + 8]], axis=0)
            put(b, pl.multiple_of(h * 16, 16), rows.astype(jnp.bfloat16))


def correlate_kernel(blk, chan, chn, spectra_count, seen, out, grouped):
    gather_feeds(lambda c, b, p: seen[c * blk + b, p], blk, chan, chn, grouped)

    def put(b, row, rows):
        out[b, pl.ds(row, 16), :] = rows

    correlate(grouped, blk, chan, chn, spectra_count, put)


def finish(get, blk, chn, feeds, out, wide):
    @pl.loop(0, blk)
    def _(b):
        for first in range(0, 2 * feeds, 128):
            value = get(b, first).astype(jnp.float32)
            wide[first // 128, pl.ds(pl.multiple_of(b * chn * 8, chn * 8), chn * 8), :] = value

    piece = min(feeds, 128)
    for i in range(8):
        for block in range(0, blk * chn, 128):
            for first in range(0, 2 * feeds, 128):
                tile = wide[first // 128, pl.ds(block * 8 + i, 128, stride=8), :].T
                for at in range(0, 128, piece):
                    part, j = divmod(first + at, feeds)
                    out[part, i, pl.ds(j, piece), pl.ds(block, 128)] = tile[at : at + piece]


def finish_kernel(blk, chn, feeds, seen, out, wide):
    finish(lambda b, first: seen[b, :, first : first + 128], blk, chn, feeds, out, wide)


def whole(count):
    return [pl.BlockSpec(memory_space=pltpu.VMEM)] * count


def on_device(chan, blk, voltages, fir_taps):
    frames = voltages.shape[1] // L
    parts = chan * blk
    chn = C // parts
    feeds = blk * 8
    spectra_count = frames * chan
    twiddle, high, low = tables()
    last = voltages[:, (frames - TAPS + 1) * L :]
    halo = lax.ppermute(last, "chan", [(a, a + 1) for a in range(chan - 1)])
    params = pltpu.CompilerParams(vmem_limit_bytes=VMEM)
    spectra = pl.pallas_call(
        functools.partial(spectra_kernel, frames, parts),
        out_shape=jax.ShapeDtypeStruct((parts, 2, chn, 128), jnp.bfloat16),
        in_specs=whole(6),
        out_specs=whole(1)[0],
        scratch_shapes=[
            pltpu.VMEM((frames * N1, 8, N2), jnp.float32),
            pltpu.VMEM((N1, 8 * frames, 2 * N2), jnp.float32),
            pltpu.VMEM((2 * C, 8 * frames), jnp.float32),
        ],
        compiler_params=params,
        name="spectra",
    )(voltages, halo, fir_taps, jnp.asarray(twiddle), jnp.asarray(high), jnp.asarray(low))
    seen = lax.all_to_all(spectra, ("chan", "blk"), split_axis=0, concat_axis=0, tiled=True)
    products = pl.pallas_call(
        functools.partial(correlate_kernel, blk, chan, chn, spectra_count),
        out_shape=jax.ShapeDtypeStruct((blk, chn * 8, 2 * feeds), jnp.bfloat16),
        in_specs=whole(1),
        out_specs=whole(1)[0],
        scratch_shapes=[pltpu.VMEM((feeds * chn, 128), jnp.float32)],
        compiler_params=params,
        name="correlate",
    )(seen)
    mine = lax.all_to_all(products, "blk", split_axis=0, concat_axis=0, tiled=True)
    return pl.pallas_call(
        functools.partial(finish_kernel, blk, chn, feeds),
        out_shape=jax.ShapeDtypeStruct((2, 8, feeds, blk * chn), jnp.float32),
        in_specs=whole(1),
        out_specs=whole(1)[0],
        scratch_shapes=[pltpu.VMEM((feeds // 64, blk * chn * 8, 128), jnp.float32)],
        compiler_params=params,
        name="finish",
    )(mine)


def solution(mesh):
    chan, blk = mesh.shape["chan"], mesh.shape["blk"]
    return jax.shard_map(
        functools.partial(on_device, chan, blk),
        mesh=mesh,
        in_specs=(P("blk", "chan"), P()),
        out_specs=P(None, "blk", None, "chan"),
        check_vma=False,
    )
```

```python
import functools
import math

import jax
import jax.numpy as jnp
import numpy as np
from jax import lax
from jax.experimental import pallas as pl
from jax.experimental.pallas import tpu as pltpu
from jax.sharding import PartitionSpec as P

TAPS = 8
L = 4096
C = 2048
N2 = 128
N1 = L // N2
HALF = C // N1
VMEM = 56 * 1024 * 1024


def tables():
    n2 = np.arange(N2)
    angle = 2.0 * np.pi * (np.arange(N1)[:, None] * n2[None, :] % L) / L
    twiddle = np.stack([np.cos(angle), np.sin(angle)]).astype(np.float32)
    angle = 2.0 * np.pi * (np.arange(HALF)[:, None] * n2[None, :] % N2) / N2
    cos, sin = np.cos(angle) / math.sqrt(L), np.sin(angle) / math.sqrt(L)
    matrix = np.block([[cos, sin], [-sin, cos]])
    high = matrix.astype(jnp.bfloat16)
    low = (matrix - high.astype(np.float64)).astype(jnp.bfloat16)
    return twiddle, high, low


def times(scale, value):
    return None if value is None else scale * value


def plus(a, b):
    return b if a is None else a if b is None else a + b


def minus(a, b):
    return a if b is None else -b if a is None else a - b


def real_dft(values):
    n = len(values)
    if n == 1:
        return [(values[0], None)]
    half = n // 2
    even, odd = real_dft(values[0::2]), real_dft(values[1::2])
    result = [None] * (half + 1)
    for k in range(half // 2 + 1):
        (er, ei), (odr, odi) = even[k], odd[k]
        if k == 0:
            tr, ti = odr, odi
        elif 4 * k == n:
            tr, ti = odi, -odr
        else:
            c, s = math.cos(2 * math.pi * k / n), math.sin(2 * math.pi * k / n)
            tr = plus(times(c, odr), times(s, odi))
            ti = minus(times(c, odi), times(s, odr))
        result[half - k] = (minus(er, tr), minus(ti, ei))
        result[k] = (plus(er, tr), plus(ei, ti))
    return result


def fir_stage(volt, halo, taps, filtered, frames):
    first, end = frames

    @pl.loop(0, N1)
    def _(n1):
        lane = pl.multiple_of(n1 * N2, N2)
        weights = [jnp.broadcast_to(taps[t : t + 1, pl.ds(lane, N2)], (8, N2)) for t in range(TAPS)]

        def frame(f):
            if f < 0:
                return halo[:, pl.ds((f + TAPS - 1) * L + lane, N2)].astype(jnp.float32)
            return volt[:, pl.ds(f * L + lane, N2)].astype(jnp.float32)

        window = [frame(f) for f in range(first - TAPS + 1, first)]
        for f in range(end - first):
            window.append(frame(first + f))
            total = weights[0] * window[f]
            for t in range(1, TAPS):
                total = total + weights[t] * window[f + t]
            filtered[(first + f) * N1 + n1] = total


def first_stage(filtered, twiddle, turned, frames):
    @pl.loop(*frames)
    def _(f):
        spectrum = real_dft([filtered[f * N1 + n1] for n1 in range(N1)])
        row = pl.multiple_of(f * 8, 8)
        for k1 in range(N1):
            if 2 * k1 <= N1:
                zr, zi = spectrum[k1]
            else:
                zr, zi = spectrum[N1 - k1]
                zi = -zi
            c = twiddle[0, k1 : k1 + 1, :]
            s = twiddle[1, k1 : k1 + 1, :]
            if k1 == 0:
                re, im = zr, jnp.zeros_like(zr)
            elif zi is None:
                re, im = c * zr, -(s * zr)
            else:
                re, im = c * zr + s * zi, c * zi - s * zr
            turned[k1, pl.ds(row, 8), pl.ds(0, N2)] = re
            turned[k1, pl.ds(row, 8), pl.ds(N2, N2)] = im


def second_stage(turned, k1, high, low):
    contract = (((1,), (1,)), ((), ()))
    wh, wl = high[...], low[...]
    z = turned[k1]
    zh = z.astype(jnp.bfloat16)
    zl = (z - zh.astype(jnp.float32)).astype(jnp.bfloat16)
    out = lax.dot_general(wl, zh, contract, preferred_element_type=jnp.float32)
    out = out + lax.dot_general(wh, zl, contract, preferred_element_type=jnp.float32)
    out = out + lax.dot_general(wh, zh, contract, preferred_element_type=jnp.float32)
    return out.astype(jnp.bfloat16)


def regroup(groups, lane):
    count = len(groups)
    d = 1
    while d < count:
        low_side = (lane & d) == 0
        result = list(groups)
        for g in range(count):
            if g & d == 0:
                a, b = groups[g], groups[g | d]
                result[g] = jnp.where(low_side, a, pltpu.roll(b, d, 1))
                result[g | d] = jnp.where(low_side, pltpu.roll(a, 128 - d, 1), b)
        groups = result
        d *= 2
    return groups


def gather_feeds(get, blk, chan, chn, grouped):
    lane = lax.broadcasted_iota(jnp.int32, (chn, 128), 1)

    @pl.loop(0, blk)
    def _(b):
        arrays = [get(c, b, p).astype(jnp.float32) for p in range(2) for c in range(chan)]
        for feed, value in enumerate(regroup(arrays, lane)):
            row = pl.multiple_of((b * 8 + feed) * chn, chn)
            grouped[pl.ds(row, chn), :] = value


def correlate(grouped, blk, chan, chn, spectra_count, put):
    feeds = blk * 8
    lane = lax.broadcasted_iota(jnp.int32, (feeds, 128), 1)
    real_lane = (lane & chan) == 0
    contract = (((1,), (1,)), ((), ()))

    def one(ch):
        value = grouped[pl.ds(ch, feeds, stride=chn), :]
        other = jnp.where(real_lane, -pltpu.roll(value, 128 - chan, 1), pltpu.roll(value, chan, 1))
        left = value.astype(jnp.bfloat16)
        right = jnp.concatenate([left, other.astype(jnp.bfloat16)], axis=0)
        out = lax.dot_general(left, right, contract, preferred_element_type=jnp.float32)
        return out * (1.0 / spectra_count)

    @pl.loop(0, chn // 2)
    def _(h):
        first, second = one(2 * h), one(2 * h + 1)
        for b in range(blk):
            rows = jnp.concatenate([first[b * 8 : b * 8 + 8], second[b * 8 : b * 8 + 8]], axis=0)
            put(b, pl.multiple_of(h * 16, 16), rows.astype(jnp.bfloat16))


def exchange_kernel(
    sizes, volt, taps, twiddle, high, low, out,
    halo, filtered, turned, sent, seen, grouped, products,
    halo_sems, send_sems, seen_sems, product_sems, out_sem,
):
    frames, chan, blk = sizes
    parts = chan * blk
    width = HALF // chan
    per = N1 // blk
    chunks, held = sent.shape[0], per // sent.shape[0]
    c, b = lax.axis_index("chan"), lax.axis_index("blk")
    barrier = pltpu.get_barrier_semaphore()

    @pl.loop(1, parts)
    def _(d):
        other = lax.rem(c * blk + b + d, parts)
        pl.semaphore_signal(
            barrier,
            inc=1,
            device_id={"chan": lax.div(other, blk), "blk": lax.rem(other, blk)},
            device_id_type=pl.DeviceIdType.MESH,
        )

    @pl.when(c == 0)
    def _():
        halo[...] = jnp.zeros_like(halo)

    late, early = (TAPS - 1, frames), (0, TAPS - 1)
    fir_stage(volt, halo, taps, filtered, late)
    pl.semaphore_wait(barrier, parts - 1)
    halo_copy = pltpu.make_async_remote_copy(
        src_ref=volt.at[:, pl.ds((frames - TAPS + 1) * L, (TAPS - 1) * L)],
        dst_ref=halo,
        send_sem=halo_sems.at[0],
        recv_sem=halo_sems.at[1],
        device_id={"chan": lax.rem(c + 1, chan), "blk": b},
        device_id_type=pl.DeviceIdType.MESH,
    )

    @pl.when(c < chan - 1)
    def _():
        halo_copy.start()

    first_stage(filtered, twiddle, turned, late)

    @pl.when(c > 0)
    def _():
        halo_copy.wait_recv()

    fir_stage(volt, halo, taps, filtered, early)
    first_stage(filtered, twiddle, turned, early)

    me = c * blk + b
    for q in range(chunks):

        @pl.loop(0, blk)
        def _(t):
            to_b = lax.rem(b + blk // 2 + t, blk)
            for kk in range(held):
                value = second_stage(turned, to_b * per + q * held + kk, high, low)
                for to_c in range(chan):
                    for p in range(2):
                        row = p * HALF + to_c * width
                        sent[q, to_c * blk + to_b, pl.ds((kk * 2 + p) * width, width), :] = value[row : row + width]
            for u in range(chan):
                to_c = lax.rem(c + u, chan)
                to = to_c * blk + to_b
                copy = pltpu.make_async_remote_copy(
                    src_ref=sent.at[q, to],
                    dst_ref=seen.at[q, me],
                    send_sem=send_sems.at[q],
                    recv_sem=seen_sems.at[q],
                    device_id={"chan": to_c, "blk": to_b},
                    device_id_type=pl.DeviceIdType.MESH,
                )
                if u == 0:
                    pl.when(to_b != b)(copy.start)

                    @pl.when(to_b == b)
                    def _():
                        pltpu.make_async_copy(sent.at[q, me], seen.at[q, me], seen_sems.at[q]).start()
                else:
                    copy.start()

    for q in range(chunks):
        pltpu.make_async_copy(seen.at[q], seen.at[q], seen_sems.at[q]).wait()
        for kk in range(held):

            def get(from_c, from_b, p):
                return seen[q, from_c * blk + from_b, pl.ds((kk * 2 + p) * width, width), :]

            index = q * held + kk

            def put(to_b, row, rows):
                products[index, to_b, pl.ds(row, 16), :] = rows

            gather_feeds(get, blk, chan, width, grouped)
            correlate(grouped, blk, chan, width, frames * chan, put)

            @pl.loop(0, blk - 1)
            def _(t):
                to_b = lax.rem(b + 1 + lax.rem(t + blk // 2 - 1, blk - 1), blk)
                pltpu.make_async_remote_copy(
                    src_ref=products.at[index, to_b],
                    dst_ref=out.at[index, b],
                    send_sem=product_sems.at[index],
                    recv_sem=out_sem,
                    device_id={"chan": c, "blk": to_b},
                    device_id_type=pl.DeviceIdType.MESH,
                ).start()

            pltpu.make_async_copy(products.at[index, b], out.at[index, b], out_sem).start()

    pltpu.make_async_copy(out, out, out_sem).wait()
    for q in range(chunks):
        part = sent.at[q, pl.ds(0, parts - 1)]
        pltpu.make_async_copy(part, part, send_sems.at[q]).wait()
    for index in range(per):
        part = products.at[index, pl.ds(0, blk - 1)]
        pltpu.make_async_copy(part, part, product_sems.at[index]).wait()

    @pl.when(c < chan - 1)
    def _():
        halo_copy.wait_send()


def finish_kernel(blk, per, width, feeds, seen, out, wide):
    @pl.loop(0, blk)
    def _(b):
        for kk in range(per):
            for first in range(0, 2 * feeds, 128):
                value = seen[kk, b, :, first : first + 128].astype(jnp.float32)
                for k2 in range(width):
                    row = pl.multiple_of((k2 * N1 + b * per + kk) * 8, 8)
                    wide[first // 128, pl.ds(row, 8), :] = value[k2 * 8 : k2 * 8 + 8]

    piece = min(feeds, 128)
    for i in range(8):
        for block in range(0, width * N1, 128):
            for first in range(0, 2 * feeds, 128):
                tile = wide[first // 128, pl.ds(block * 8 + i, 128, stride=8), :].T
                for at in range(0, 128, piece):
                    part, j = divmod(first + at, feeds)
                    out[part, i, pl.ds(j, piece), pl.ds(block, 128)] = tile[at : at + piece]


def whole(count):
    return [pl.BlockSpec(memory_space=pltpu.VMEM)] * count


def on_device(chan, blk, voltages, fir_taps):
    frames = voltages.shape[1] // L
    parts = chan * blk
    feeds = blk * 8
    per, width = N1 // blk, HALF // chan
    chunks = min(per, 2)
    rows = 2 * width * per // chunks
    twiddle, high, low = tables()
    dma = pltpu.SemaphoreType.DMA
    mine = pl.pallas_call(
        functools.partial(exchange_kernel, (frames, chan, blk)),
        out_shape=jax.ShapeDtypeStruct((per, blk, width * 8, 2 * feeds), jnp.bfloat16),
        in_specs=whole(5),
        out_specs=pl.BlockSpec(memory_space=pl.ANY),
        scratch_shapes=[
            pltpu.VMEM((8, (TAPS - 1) * L), jnp.bfloat16),
            pltpu.VMEM((frames * N1, 8, N2), jnp.float32),
            pltpu.VMEM((N1, 8 * frames, 2 * N2), jnp.float32),
            pltpu.VMEM((chunks, parts, rows, 128), jnp.bfloat16),
            pltpu.VMEM((chunks, parts, rows, 128), jnp.bfloat16),
            pltpu.VMEM((feeds * width, 128), jnp.float32),
            pltpu.VMEM((per, blk, width * 8, 2 * feeds), jnp.bfloat16),
            dma((2,)),
            dma((chunks,)),
            dma((chunks,)),
            dma((per,)),
            dma,
        ],
        compiler_params=pltpu.CompilerParams(vmem_limit_bytes=VMEM, collective_id=0, has_side_effects=True),
        name="exchange",
    )(voltages, fir_taps, jnp.asarray(twiddle), jnp.asarray(high), jnp.asarray(low))
    return pl.pallas_call(
        functools.partial(finish_kernel, blk, per, width, feeds),
        out_shape=jax.ShapeDtypeStruct((2, 8, feeds, width * N1), jnp.float32),
        in_specs=whole(1),
        out_specs=whole(1)[0],
        scratch_shapes=[pltpu.VMEM((feeds // 64, width * N1 * 8, 128), jnp.float32)],
        compiler_params=pltpu.CompilerParams(vmem_limit_bytes=VMEM),
        name="finish",
    )(mine)


def solution(mesh):
    chan, blk = mesh.shape["chan"], mesh.shape["blk"]
    return jax.shard_map(
        functools.partial(on_device, chan, blk),
        mesh=mesh,
        in_specs=(P("blk", "chan"), P()),
        out_specs=P(None, "blk", None, "chan"),
        check_vma=False,
    )
```

```python
import functools
import math

import jax
import jax.numpy as jnp
import numpy as np
from jax import lax
from jax.experimental import pallas as pl
from jax.experimental.pallas import tpu as pltpu
from jax.sharding import PartitionSpec as P

TAPS = 8
L = 4096
C = 2048
N2 = 128
N1 = L // N2
HALF = C // N1
VMEM = 56 * 1024 * 1024


def tables():
    n2 = np.arange(N2)
    angle = 2.0 * np.pi * (np.arange(N1)[:, None] * n2[None, :] % L) / L
    twiddle = np.stack([np.cos(angle), np.sin(angle)]).astype(np.float32)
    angle = 2.0 * np.pi * (np.arange(HALF)[:, None] * n2[None, :] % N2) / N2
    cos, sin = np.cos(angle) / math.sqrt(L), np.sin(angle) / math.sqrt(L)
    matrix = np.block([[cos, sin], [-sin, cos]])
    high = matrix.astype(jnp.bfloat16)
    low = (matrix - high.astype(np.float64)).astype(jnp.bfloat16)
    return twiddle, high, low


def times(scale, value):
    return None if value is None else scale * value


def plus(a, b):
    return b if a is None else a if b is None else a + b


def minus(a, b):
    return a if b is None else -b if a is None else a - b


def real_dft(values):
    n = len(values)
    if n == 1:
        return [(values[0], None)]
    half = n // 2
    even, odd = real_dft(values[0::2]), real_dft(values[1::2])
    result = [None] * (half + 1)
    for k in range(half // 2 + 1):
        (er, ei), (odr, odi) = even[k], odd[k]
        if k == 0:
            tr, ti = odr, odi
        elif 4 * k == n:
            tr, ti = odi, -odr
        else:
            c, s = math.cos(2 * math.pi * k / n), math.sin(2 * math.pi * k / n)
            tr = plus(times(c, odr), times(s, odi))
            ti = minus(times(c, odi), times(s, odr))
        result[half - k] = (minus(er, tr), minus(ti, ei))
        result[k] = (plus(er, tr), plus(ei, ti))
    return result


def fir_stage(volt, halo, taps, filtered, frames):
    first, end = frames

    @pl.loop(0, N1)
    def _(n1):
        lane = pl.multiple_of(n1 * N2, N2)
        weights = [jnp.broadcast_to(taps[t : t + 1, pl.ds(lane, N2)], (8, N2)) for t in range(TAPS)]

        def frame(f):
            if f < 0:
                return halo[:, pl.ds((f + TAPS - 1) * L + lane, N2)].astype(jnp.float32)
            return volt[:, pl.ds(f * L + lane, N2)].astype(jnp.float32)

        window = [frame(f) for f in range(first - TAPS + 1, first)]
        for f in range(end - first):
            window.append(frame(first + f))
            total = weights[0] * window[f]
            for t in range(1, TAPS):
                total = total + weights[t] * window[f + t]
            filtered[(first + f) * N1 + n1] = total


def first_stage(filtered, twiddle, turned, frames):
    @pl.loop(*frames)
    def _(f):
        spectrum = real_dft([filtered[f * N1 + n1] for n1 in range(N1)])
        row = pl.multiple_of(f * 8, 8)
        for k1 in range(N1):
            if 2 * k1 <= N1:
                zr, zi = spectrum[k1]
            else:
                zr, zi = spectrum[N1 - k1]
                zi = -zi
            c = twiddle[0, k1 : k1 + 1, :]
            s = twiddle[1, k1 : k1 + 1, :]
            if k1 == 0:
                re, im = zr, jnp.zeros_like(zr)
            elif zi is None:
                re, im = c * zr, -(s * zr)
            else:
                re, im = c * zr + s * zi, c * zi - s * zr
            turned[k1, pl.ds(row, 8), pl.ds(0, N2)] = re
            turned[k1, pl.ds(row, 8), pl.ds(N2, N2)] = im


def second_stage(turned, k1, high, low):
    contract = (((1,), (1,)), ((), ()))
    wh, wl = high[...], low[...]
    z = turned[k1]
    zh = z.astype(jnp.bfloat16)
    zl = (z - zh.astype(jnp.float32)).astype(jnp.bfloat16)
    out = lax.dot_general(wl, zh, contract, preferred_element_type=jnp.float32)
    out = out + lax.dot_general(wh, zl, contract, preferred_element_type=jnp.float32)
    out = out + lax.dot_general(wh, zh, contract, preferred_element_type=jnp.float32)
    return out.astype(jnp.bfloat16)


def regroup(groups, lane):
    count = len(groups)
    d = 1
    while d < count:
        low_side = (lane & d) == 0
        result = list(groups)
        for g in range(count):
            if g & d == 0:
                a, b = groups[g], groups[g | d]
                result[g] = jnp.where(low_side, a, pltpu.roll(b, d, 1))
                result[g | d] = jnp.where(low_side, pltpu.roll(a, 128 - d, 1), b)
        groups = result
        d *= 2
    return groups


def gather_feeds(get, blk, chan, width, place, grouped):
    lane = lax.broadcasted_iota(jnp.int32, (width, 128), 1)

    @pl.loop(0, blk)
    def _(b):
        arrays = [get(c, b, p).astype(jnp.float32) for p in range(2) for c in range(chan)]
        for feed, value in enumerate(regroup(arrays, lane)):
            row = pl.multiple_of((place(b) * 8 + feed) * width, width)
            grouped[pl.ds(row, width), :] = value


def sides(grouped, ch, feeds, width, chan):
    lane = lax.broadcasted_iota(jnp.int32, (feeds, 128), 1)
    value = grouped[pl.ds(ch, feeds, stride=width), :]
    other = jnp.where((lane & chan) == 0, -pltpu.roll(value, 128 - chan, 1), pltpu.roll(value, chan, 1))
    return value.astype(jnp.bfloat16), other.astype(jnp.bfloat16)


def product(left, right):
    return lax.dot_general(left, right, (((1,), (1,)), ((), ())), preferred_element_type=jnp.float32)


def paired(lefts, rights):
    zero = jnp.zeros_like(rights[0])
    right = jnp.concatenate(
        [jnp.concatenate([rights[0], zero], axis=1), jnp.concatenate([zero, rights[1]], axis=1)], axis=0
    )
    return product(jnp.concatenate(lefts, axis=1), right)


def correlate(grouped, nearby, half, chan, width, spectra_count, near, far):
    near_feeds = half * 8
    feeds = 2 * near_feeds
    scale = 1.0 / spectra_count

    @pl.loop(0, width // 4)
    def _(quad):
        far_rows, own_rows, full_rows = [], [], []
        for pair in range(2):
            lefts, rights, own_lefts, own_rights, full = [], [], [], [], []
            for one in range(2):
                ch = quad * 4 + pair * 2 + one
                value, other = sides(grouped, ch, feeds, width, chan)
                right = jnp.concatenate([value[:near_feeds], other[:near_feeds]], axis=0)
                rest = jnp.concatenate([value[near_feeds:], other[near_feeds:]], axis=0)
                full.append(product(value[:near_feeds], jnp.concatenate([right, rest], axis=0)) * scale)
                lefts.append(value[near_feeds:])
                rights.append(right)
                value, other = sides(nearby, ch, near_feeds, width, chan)
                own_lefts.append(value)
                own_rights.append(jnp.concatenate([value, other], axis=0))
            full_rows.append(full)
            far_rows.append(paired(lefts, rights) * scale)
            own_rows.append(paired(own_lefts, own_rights) * scale)
        for b in range(half):
            cut = slice(b * 8, b * 8 + 8)

            def put(ref, row, first, second):
                rows = jnp.concatenate([first[cut], second[cut]], axis=0)
                ref[b, pl.ds(pl.multiple_of(row, 16), 16), :] = rows.astype(jnp.bfloat16)

            for pair in range(2):
                put(near, (quad * 2 + pair) * 16, *full_rows[pair])
            put(near, width * 8 + quad * 16, *own_rows)
            put(far, quad * 16, *far_rows)


def exchange_kernel(
    sizes, volt, taps, twiddle, high, low, out_near, out_far,
    halo, filtered, turned, sent, seen, seen_near, grouped, nearby, near, far,
    halo_sems, send_sems, seen_sems, product_sems, out_sems,
):
    frames, chan, blk = sizes
    parts, half = chan * blk, blk // 2
    width = HALF // chan
    per = N1 // blk
    chunks, held = sent.shape[0], per // sent.shape[0]
    c, b = lax.axis_index("chan"), lax.axis_index("blk")
    side, spot = lax.div(b, half), lax.rem(b, half)
    barrier = pltpu.get_barrier_semaphore()

    def remote(src, dst, send_sem, recv_sem, to_c, to_b):
        return pltpu.make_async_remote_copy(
            src_ref=src,
            dst_ref=dst,
            send_sem=send_sem,
            recv_sem=recv_sem,
            device_id={"chan": to_c, "blk": to_b},
            device_id_type=pl.DeviceIdType.MESH,
        )

    @pl.loop(1, parts)
    def _(d):
        other = lax.rem(c * blk + b + d, parts)
        pl.semaphore_signal(
            barrier,
            inc=1,
            device_id={"chan": lax.div(other, blk), "blk": lax.rem(other, blk)},
            device_id_type=pl.DeviceIdType.MESH,
        )

    @pl.when(c == 0)
    def _():
        halo[...] = jnp.zeros_like(halo)

    late, early = (TAPS - 1, frames), (0, TAPS - 1)
    fir_stage(volt, halo, taps, filtered, late)
    pl.semaphore_wait(barrier, parts - 1)
    last = volt.at[:, pl.ds((frames - TAPS + 1) * L, (TAPS - 1) * L)]
    halo_copy = remote(last, halo, halo_sems.at[0], halo_sems.at[1], lax.rem(c + 1, chan), b)

    @pl.when(c < chan - 1)
    def _():
        halo_copy.start()

    first_stage(filtered, twiddle, turned, late)

    @pl.when(c > 0)
    def _():
        halo_copy.wait_recv()

    fir_stage(volt, halo, taps, filtered, early)
    first_stage(filtered, twiddle, turned, early)

    for q in range(chunks):

        @pl.loop(0, half)
        def _(t):
            at = lax.rem(spot + 1 + t, half)
            near_b, far_b = side * half + at, (1 - side) * half + at
            for to_b in (far_b, near_b):
                for kk in range(held):
                    value = second_stage(turned, to_b * per + q * held + kk, high, low)
                    for to_c in range(chan):
                        for p in range(2):
                            row = p * HALF + to_c * width
                            place = pl.ds((kk * 2 + p) * width, width)
                            sent[q, to_c * blk + to_b, place, :] = value[row : row + width]
                if to_b is far_b:
                    for u in range(chan):
                        to_c = lax.rem(c + u, chan)
                        block = sent.at[q, to_c * blk + far_b]
                        remote(
                            block, seen.at[q, c * blk + b], send_sems.at[0, q], seen_sems.at[0, q], to_c, far_b
                        ).start()
            for u in range(chan):
                to_c = lax.rem(c + u, chan)
                for kind, to_b, dst in (
                    (0, near_b, seen.at[q, c * blk + b]),
                    (1, far_b, seen_near.at[q, c * half + spot]),
                ):
                    block = sent.at[q, to_c * blk + to_b]
                    copy = remote(block, dst, send_sems.at[kind, q], seen_sems.at[kind, q], to_c, near_b)
                    if u == 0:
                        pl.when(near_b != b)(copy.start)
                        pl.when(near_b == b)(pltpu.make_async_copy(block, dst, seen_sems.at[kind, q]).start)
                    else:
                        copy.start()

    for q in range(chunks):
        for kind, ref in enumerate((seen, seen_near)):
            pltpu.make_async_copy(ref.at[q], ref.at[q], seen_sems.at[kind, q]).wait()
        for kk in range(held):

            def get(from_c, from_b, p):
                return seen[q, from_c * blk + from_b, pl.ds((kk * 2 + p) * width, width), :]

            def get_near(from_c, at, p):
                return seen_near[q, from_c * half + at, pl.ds((kk * 2 + p) * width, width), :]

            index = q * held + kk
            gather_feeds(get, blk, chan, width, lambda from_b: lax.rem(from_b + side * half, blk), grouped)
            gather_feeds(get_near, half, chan, width, lambda at: at, nearby)
            correlate(grouped, nearby, half, chan, width, frames * chan, near.at[index], far.at[index])

            @pl.loop(0, half)
            def _(t):
                at = lax.rem(spot + 1 + t, half)
                near_b, far_b = side * half + at, (1 - side) * half + at
                remote(
                    far.at[index, at], out_far.at[index, spot], product_sems.at[1, index], out_sems.at[1], c, far_b
                ).start()
                copy = remote(
                    near.at[index, at], out_near.at[index, spot], product_sems.at[0, index], out_sems.at[0], c, near_b
                )
                pl.when(at != spot)(copy.start)

            pltpu.make_async_copy(near.at[index, spot], out_near.at[index, spot], out_sems.at[0]).start()

    pltpu.make_async_copy(out_near, out_near, out_sems.at[0]).wait()
    pltpu.make_async_copy(out_far, out_far, out_sems.at[1]).wait()
    for q in range(chunks):
        for kind, count in enumerate((parts, chan * half)):
            part = sent.at[q, pl.ds(0, count - 1)]
            pltpu.make_async_copy(part, part, send_sems.at[kind, q]).wait()
    for index in range(per):
        part = near.at[index, pl.ds(0, half - 1)]
        pltpu.make_async_copy(part, part, product_sems.at[0, index]).wait()
        pltpu.make_async_copy(far.at[index], far.at[index], product_sems.at[1, index]).wait()

    @pl.when(c < chan - 1)
    def _():
        halo_copy.wait_send()


def join(first, second, feeds):
    if feeds % 128 == 0:
        return [
            jnp.concatenate([first[:, cut], second[:, cut]], axis=1)
            for cut in (slice(0, feeds), slice(feeds, 2 * feeds))
        ]
    lane = lax.broadcasted_iota(jnp.int32, first.shape, 1)
    low_side = lane < feeds
    return [
        jnp.where(low_side, first, pltpu.roll(second, feeds, 1)),
        jnp.where(low_side, pltpu.roll(first, feeds, 1), second),
    ]


def finish_kernel(blk, per, width, feeds, near, far, out, wide):
    half = blk // 2
    side = lax.div(lax.axis_index("blk"), half)

    def put(k2, k1, rows):
        row = pl.multiple_of((k2 * N1 + k1) * 8, 8)
        for first in range(0, 2 * feeds, 128):
            wide[first // 128, pl.ds(row, 8), :] = rows[:, first : first + 128]

    @pl.loop(0, half)
    def _(at):
        near_b, far_b = side * half + at, (1 - side) * half + at
        for kk in range(per):
            value = near[kk, at].astype(jnp.float32)
            other = far[kk, at].astype(jnp.float32)
            for k2 in range(width):
                put(k2, near_b * per + kk, value[k2 * 8 : k2 * 8 + 8])
            for pair in range(width // 2):
                own = value[(width + pair) * 8 : (width + pair) * 8 + 8]
                for one, rows in enumerate(join(own, other[pair * 8 : pair * 8 + 8], feeds)):
                    put(2 * pair + one, far_b * per + kk, rows)

    count = feeds // 2
    piece = min(count, 128)
    for i in range(8):
        for block in range(0, width * N1, 128):
            for first in range(0, 2 * feeds, 128):
                tile = wide[first // 128, pl.ds(block * 8 + i, 128, stride=8), :].T
                for at in range(0, 128, piece):
                    which, rest = divmod(first + at, feeds)
                    part, j = divmod(rest, count)
                    start = (side if which == 0 else 1 - side) * count + j
                    out[part, i, pl.ds(pl.multiple_of(start, piece), piece), pl.ds(block, 128)] = tile[at : at + piece]


def whole(count):
    return [pl.BlockSpec(memory_space=pltpu.VMEM)] * count


def on_device(chan, blk, voltages, fir_taps):
    frames = voltages.shape[1] // L
    parts, half = chan * blk, blk // 2
    feeds = blk * 8
    per, width = N1 // blk, HALF // chan
    chunks = min(per, 2)
    rows = 2 * width * per // chunks
    twiddle, high, low = tables()
    dma = pltpu.SemaphoreType.DMA
    any_place = pl.BlockSpec(memory_space=pl.ANY)
    near = (per, half, width * 12, 2 * feeds)
    far = (per, half, width * 4, 2 * feeds)
    mine = pl.pallas_call(
        functools.partial(exchange_kernel, (frames, chan, blk)),
        out_shape=[jax.ShapeDtypeStruct(near, jnp.bfloat16), jax.ShapeDtypeStruct(far, jnp.bfloat16)],
        in_specs=whole(5),
        out_specs=[any_place, any_place],
        scratch_shapes=[
            pltpu.VMEM((8, (TAPS - 1) * L), jnp.bfloat16),
            pltpu.VMEM((frames * N1, 8, N2), jnp.float32),
            pltpu.VMEM((N1, 8 * frames, 2 * N2), jnp.float32),
            pltpu.VMEM((chunks, parts, rows, 128), jnp.bfloat16),
            pltpu.VMEM((chunks, parts, rows, 128), jnp.bfloat16),
            pltpu.VMEM((chunks, parts // 2, rows, 128), jnp.bfloat16),
            pltpu.VMEM((feeds * width, 128), jnp.float32),
            pltpu.VMEM((feeds // 2 * width, 128), jnp.float32),
            pltpu.VMEM(near, jnp.bfloat16),
            pltpu.VMEM(far, jnp.bfloat16),
            dma((2,)),
            dma((2, chunks)),
            dma((2, chunks)),
            dma((2, per)),
            dma((2,)),
        ],
        compiler_params=pltpu.CompilerParams(vmem_limit_bytes=VMEM, collective_id=0, has_side_effects=True),
        name="exchange",
    )(voltages, fir_taps, jnp.asarray(twiddle), jnp.asarray(high), jnp.asarray(low))
    return pl.pallas_call(
        functools.partial(finish_kernel, blk, per, width, feeds),
        out_shape=jax.ShapeDtypeStruct((2, 8, feeds, width * N1), jnp.float32),
        in_specs=whole(2),
        out_specs=whole(1)[0],
        scratch_shapes=[pltpu.VMEM((feeds // 64, width * N1 * 8, 128), jnp.float32)],
        compiler_params=pltpu.CompilerParams(vmem_limit_bytes=VMEM),
        name="finish",
    )(*mine)


def solution(mesh):
    chan, blk = mesh.shape["chan"], mesh.shape["blk"]
    return jax.shard_map(
        functools.partial(on_device, chan, blk),
        mesh=mesh,
        in_specs=(P("blk", "chan"), P()),
        out_specs=P(None, "blk", None, "chan"),
        check_vma=False,
    )
```

```python
import functools
import math

import jax
import jax.numpy as jnp
import numpy as np
from jax import lax
from jax.experimental import pallas as pl
from jax.experimental.pallas import tpu as pltpu
from jax.sharding import PartitionSpec as P

TAPS = 8
L = 4096
C = 2048
N2 = 128
N1 = L // N2
HALF = C // N1
VMEM = 56 * 1024 * 1024


def tables():
    n2 = np.arange(N2)
    angle = 2.0 * np.pi * (np.arange(N1)[:, None] * n2[None, :] % L) / L
    twiddle = np.stack([np.cos(angle), np.sin(angle)]).astype(np.float32)
    angle = 2.0 * np.pi * (np.arange(HALF)[:, None] * n2[None, :] % N2) / N2
    cos, sin = np.cos(angle) / math.sqrt(L), np.sin(angle) / math.sqrt(L)
    matrix = np.block([[cos, sin], [-sin, cos]])
    high = matrix.astype(jnp.bfloat16)
    low = (matrix - high.astype(np.float64)).astype(jnp.bfloat16)
    return twiddle, np.concatenate([low, high])


def times(scale, value):
    return None if value is None else scale * value


def plus(a, b):
    return b if a is None else a if b is None else a + b


def minus(a, b):
    return a if b is None else -b if a is None else a - b


def real_dft(values):
    n = len(values)
    if n == 1:
        return [(values[0], None)]
    half = n // 2
    even, odd = real_dft(values[0::2]), real_dft(values[1::2])
    result = [None] * (half + 1)
    for k in range(half // 2 + 1):
        (er, ei), (odr, odi) = even[k], odd[k]
        if k == 0:
            tr, ti = odr, odi
        elif 4 * k == n:
            tr, ti = odi, -odr
        else:
            c, s = math.cos(2 * math.pi * k / n), math.sin(2 * math.pi * k / n)
            tr = plus(times(c, odr), times(s, odi))
            ti = minus(times(c, odi), times(s, odr))
        result[half - k] = (minus(er, tr), minus(ti, ei))
        result[k] = (plus(er, tr), plus(ei, ti))
    return result


def fir_stage(volt, halo, taps, filtered, frames):
    first, end = frames

    @pl.loop(0, N1)
    def _(n1):
        lane = pl.multiple_of(n1 * N2, N2)
        weights = [jnp.broadcast_to(taps[t : t + 1, pl.ds(lane, N2)], (8, N2)) for t in range(TAPS)]

        def frame(f):
            if f < 0:
                return halo[:, pl.ds((f + TAPS - 1) * L + lane, N2)].astype(jnp.float32)
            return volt[:, pl.ds(f * L + lane, N2)].astype(jnp.float32)

        window = [frame(f) for f in range(first - TAPS + 1, first)]
        for f in range(end - first):
            window.append(frame(first + f))
            total = weights[0] * window[f]
            for t in range(1, TAPS):
                total = total + weights[t] * window[f + t]
            filtered[(first + f) * N1 + n1] = total


def first_stage(filtered, twiddle, turned, part, frames):
    @pl.loop(0, frames)
    def _(f):
        spectrum = real_dft([filtered[(part * frames + f) * N1 + n1] for n1 in range(N1)])
        rows = pl.ds(pl.multiple_of(f * 8, 8), 8)
        for k1 in range(N1):
            if 2 * k1 <= N1:
                zr, zi = spectrum[k1]
            else:
                zr, zi = spectrum[N1 - k1]
                zi = -zi
            c = twiddle[0, k1 : k1 + 1, :]
            s = twiddle[1, k1 : k1 + 1, :]
            if k1 == 0:
                re, im = zr, jnp.zeros_like(zr)
            elif zi is None:
                re, im = c * zr, -(s * zr)
            else:
                re, im = c * zr + s * zi, c * zi - s * zr
            turned[part * N1 + k1, rows, pl.ds(0, N2)] = re
            turned[part * N1 + k1, rows, pl.ds(N2, N2)] = im


def second_stage(turned, first, second, table):
    contract = (((1,), (1,)), ((), ()))
    z = jnp.concatenate([turned[first], turned[second]], axis=0)
    zh = z.astype(jnp.bfloat16)
    zl = (z - zh.astype(jnp.float32)).astype(jnp.bfloat16)
    both = lax.dot_general(table[...], zh, contract, preferred_element_type=jnp.float32)
    rest = lax.dot_general(table[2 * HALF :], zl, contract, preferred_element_type=jnp.float32)
    out = both[2 * HALF :] + (both[: 2 * HALF] + rest)
    return [value.astype(jnp.bfloat16) for value in join(out[:HALF], out[HALF:], 64)]


def regroup(groups, lane):
    count = len(groups)
    d = 1
    while d < count:
        low_side = (lane & d) == 0
        result = list(groups)
        for g in range(count):
            if g & d == 0:
                a, b = groups[g], groups[g | d]
                result[g] = jnp.where(low_side, a, pltpu.roll(b, d, 1))
                result[g | d] = jnp.where(low_side, pltpu.roll(a, 128 - d, 1), b)
        groups = result
        d *= 2
    return groups


def gather_feeds(get, blk, chan, width, place, grouped):
    lane = lax.broadcasted_iota(jnp.int32, (width, 128), 1)

    @pl.loop(0, blk)
    def _(b):
        arrays = [get(c, b, part).astype(jnp.float32) for part in range(2) for c in range(chan)]
        for feed, value in enumerate(regroup(arrays, lane)):
            row = pl.multiple_of((place(b) * 8 + feed) * width, width)
            grouped[pl.ds(row, width), :] = value


def sides(grouped, ch, feeds, width):
    lane = lax.broadcasted_iota(jnp.int32, (feeds, 128), 1)
    value = grouped[pl.ds(ch, feeds, stride=width), :]
    other = pltpu.roll(value, 64, 1)
    other = jnp.where(lane < 64, -other, other)
    return value.astype(jnp.bfloat16), other.astype(jnp.bfloat16)


def product(left, right):
    return lax.dot_general(left, right, (((1,), (1,)), ((), ())), preferred_element_type=jnp.float32)


def paired(lefts, rights):
    zero = jnp.zeros_like(rights[0])
    right = jnp.concatenate(
        [jnp.concatenate([rights[0], zero], axis=1), jnp.concatenate([zero, rights[1]], axis=1)], axis=0
    )
    return product(jnp.concatenate(lefts, axis=1), right)


def correlate(grouped, nearby, half, width, spectra_count, near, far):
    near_feeds = half * 8
    feeds = 2 * near_feeds
    scale = 1.0 / spectra_count

    @pl.loop(0, width // 4)
    def _(quad):
        far_rows, own_rows, full_rows = [], [], []
        for pair in range(2):
            lefts, rights, own_lefts, own_rights, full = [], [], [], [], []
            for one in range(2):
                ch = quad * 4 + pair * 2 + one
                value, other = sides(grouped, ch, feeds, width)
                right = jnp.concatenate([value[:near_feeds], other[:near_feeds]], axis=0)
                rest = jnp.concatenate([value[near_feeds:], other[near_feeds:]], axis=0)
                full.append(product(value[:near_feeds], jnp.concatenate([right, rest], axis=0)) * scale)
                lefts.append(value[near_feeds:])
                rights.append(right)
                value, other = sides(nearby, ch, near_feeds, width)
                own_lefts.append(value)
                own_rights.append(jnp.concatenate([value, other], axis=0))
            full_rows.append(full)
            far_rows.append(paired(lefts, rights) * scale)
            own_rows.append(paired(own_lefts, own_rights) * scale)
        for b in range(half):
            cut = slice(b * 8, b * 8 + 8)

            def put(ref, row, first, second):
                rows = jnp.concatenate([first[cut], second[cut]], axis=0)
                ref[b, pl.ds(pl.multiple_of(row, 16), 16), :] = rows.astype(jnp.bfloat16)

            for pair in range(2):
                put(near, (quad * 2 + pair) * 16, *full_rows[pair])
            put(near, width * 8 + quad * 16, *own_rows)
            put(far, quad * 16, *far_rows)


def exchange_kernel(
    sizes, volt, taps, twiddle, table, out_near, out_far,
    halo, filtered, turned, sent_late, sent, seen_late, seen, near_late, seen_near, grouped, nearby, near, far,
    halo_sems, send_sems, seen_sems, product_sems, out_sems,
):
    frames, chan, blk = sizes
    parts, half = chan * blk, blk // 2
    width = HALF // chan
    per = N1 // blk
    chunks, held = sent.shape[0], per // sent.shape[0]
    c, b = lax.axis_index("chan"), lax.axis_index("blk")
    side, spot = lax.div(b, half), lax.rem(b, half)
    barrier = pltpu.get_barrier_semaphore()

    def remote(src, dst, send_sem, recv_sem, to_c, to_b):
        return pltpu.make_async_remote_copy(
            src_ref=src,
            dst_ref=dst,
            send_sem=send_sem,
            recv_sem=recv_sem,
            device_id={"chan": to_c, "blk": to_b},
            device_id_type=pl.DeviceIdType.MESH,
        )

    @pl.loop(1, parts)
    def _(d):
        other = lax.rem(c * blk + b + d, parts)
        pl.semaphore_signal(
            barrier,
            inc=1,
            device_id={"chan": lax.div(other, blk), "blk": lax.rem(other, blk)},
            device_id_type=pl.DeviceIdType.MESH,
        )

    @pl.when(c == 0)
    def _():
        halo[...] = jnp.zeros_like(halo)

    def send(part, q, slot, held, sent, seen, seen_near):
        @pl.loop(0, half)
        def _(t):
            at = lax.rem(spot + 1 + t, half)
            near_b, far_b = side * half + at, (1 - side) * half + at
            for to_b in (far_b, near_b):
                base = part * N1 + to_b * per + q * held
                for first in range(0, held, 2):
                    second = min(first + 1, held - 1)
                    values = second_stage(turned, base + first, base + second, table)
                    for kk in range(first, second + 1):
                        for to_c in range(chan):
                            rows = pl.ds(kk * width, width)
                            sent[q, to_c * blk + to_b, rows, :] = values[kk - first][to_c * width : (to_c + 1) * width]
                if to_b is far_b:
                    for u in range(chan):
                        to_c = lax.rem(c + u, chan)
                        block = sent.at[q, to_c * blk + far_b]
                        dst = seen.at[q, c * blk + b]
                        remote(block, dst, send_sems.at[0, slot], seen_sems.at[0, slot], to_c, far_b).start()
            for u in range(chan):
                to_c = lax.rem(c + u, chan)
                for kind, to_b, dst in (
                    (0, near_b, seen.at[q, c * blk + b]),
                    (1, far_b, seen_near.at[q, c * half + spot]),
                ):
                    block = sent.at[q, to_c * blk + to_b]
                    copy = remote(block, dst, send_sems.at[kind, slot], seen_sems.at[kind, slot], to_c, near_b)
                    if u == 0:
                        pl.when(near_b != b)(copy.start)
                        pl.when(near_b == b)(pltpu.make_async_copy(block, dst, seen_sems.at[kind, slot]).start)
                    else:
                        copy.start()

    count = frames // 2
    fir_stage(volt, halo, taps, filtered, (count, frames))
    pl.semaphore_wait(barrier, parts - 1)
    last = volt.at[:, pl.ds((frames - TAPS + 1) * L, (TAPS - 1) * L)]
    halo_copy = remote(last, halo, halo_sems.at[0], halo_sems.at[1], lax.rem(c + 1, chan), b)

    @pl.when(c < chan - 1)
    def _():
        halo_copy.start()

    first_stage(filtered, twiddle, turned, 1, count)
    send(1, 0, 0, per, sent_late, seen_late, near_late)

    @pl.when(c > 0)
    def _():
        halo_copy.wait_recv()

    fir_stage(volt, halo, taps, filtered, (0, count))
    first_stage(filtered, twiddle, turned, 0, count)
    for q in range(chunks):
        send(0, q, 1 + q, held, sent, seen, seen_near)

    def arrived(ref, kind, q, slot):
        pltpu.make_async_copy(ref.at[q], ref.at[q], seen_sems.at[kind, slot]).wait()

    arrived(seen_late, 0, 0, 0)
    arrived(near_late, 1, 0, 0)
    for q in range(chunks):
        arrived(seen, 0, q, 1 + q)
        arrived(seen_near, 1, q, 1 + q)
        for kk in range(held):
            index = q * held + kk

            def block(late, early, source, part):
                if part == 1:
                    return late[0, source, pl.ds(index * width, width), :]
                return early[q, source, pl.ds(kk * width, width), :]

            def get(from_c, from_b, part):
                return block(seen_late, seen, from_c * blk + from_b, part)

            def get_near(from_c, at, part):
                return block(near_late, seen_near, from_c * half + at, part)

            gather_feeds(get, blk, chan, width, lambda from_b: lax.rem(from_b + side * half, blk), grouped)
            gather_feeds(get_near, half, chan, width, lambda at: at, nearby)
            correlate(grouped, nearby, half, width, frames * chan, near.at[index], far.at[index])

            @pl.loop(0, half)
            def _(t):
                at = lax.rem(spot + 1 + t, half)
                near_b, far_b = side * half + at, (1 - side) * half + at
                remote(
                    far.at[index, at], out_far.at[index, spot], product_sems.at[1, index], out_sems.at[1], c, far_b
                ).start()
                copy = remote(
                    near.at[index, at], out_near.at[index, spot], product_sems.at[0, index], out_sems.at[0], c, near_b
                )
                pl.when(at != spot)(copy.start)

            pltpu.make_async_copy(near.at[index, spot], out_near.at[index, spot], out_sems.at[0]).start()

    pltpu.make_async_copy(out_near, out_near, out_sems.at[0]).wait()
    pltpu.make_async_copy(out_far, out_far, out_sems.at[1]).wait()
    for slot in range(1 + chunks):
        ref, q = (sent_late, 0) if slot == 0 else (sent, slot - 1)
        for kind, number in enumerate((parts, chan * half)):
            piece = ref.at[q, pl.ds(0, number - 1)]
            pltpu.make_async_copy(piece, piece, send_sems.at[kind, slot]).wait()
    for index in range(per):
        piece = near.at[index, pl.ds(0, half - 1)]
        pltpu.make_async_copy(piece, piece, product_sems.at[0, index]).wait()
        pltpu.make_async_copy(far.at[index], far.at[index], product_sems.at[1, index]).wait()

    @pl.when(c < chan - 1)
    def _():
        halo_copy.wait_send()


def join(first, second, feeds):
    if feeds % 128 == 0:
        return [
            jnp.concatenate([first[:, cut], second[:, cut]], axis=1)
            for cut in (slice(0, feeds), slice(feeds, 2 * feeds))
        ]
    lane = lax.broadcasted_iota(jnp.int32, first.shape, 1)
    low_side = lane < feeds
    return [
        jnp.where(low_side, first, pltpu.roll(second, feeds, 1)),
        jnp.where(low_side, pltpu.roll(first, feeds, 1), second),
    ]


def finish_kernel(blk, per, width, feeds, near, far, out, wide):
    half = blk // 2
    side = lax.div(lax.axis_index("blk"), half)

    def put(k2, k1, rows):
        row = pl.multiple_of((k2 * N1 + k1) * 8, 8)
        for first in range(0, 2 * feeds, 128):
            wide[first // 128, pl.ds(row, 8), :] = rows[:, first : first + 128]

    @pl.loop(0, half)
    def _(at):
        near_b, far_b = side * half + at, (1 - side) * half + at
        for kk in range(per):
            value = near[kk, at].astype(jnp.float32)
            other = far[kk, at].astype(jnp.float32)
            for k2 in range(width):
                put(k2, near_b * per + kk, value[k2 * 8 : k2 * 8 + 8])
            for pair in range(width // 2):
                own = value[(width + pair) * 8 : (width + pair) * 8 + 8]
                for one, rows in enumerate(join(own, other[pair * 8 : pair * 8 + 8], feeds)):
                    put(2 * pair + one, far_b * per + kk, rows)

    count = feeds // 2
    piece = min(count, 128)
    for i in range(8):
        for block in range(0, width * N1, 128):
            for first in range(0, 2 * feeds, 128):
                tile = wide[first // 128, pl.ds(block * 8 + i, 128, stride=8), :].T
                for at in range(0, 128, piece):
                    which, rest = divmod(first + at, feeds)
                    part, j = divmod(rest, count)
                    start = (side if which == 0 else 1 - side) * count + j
                    out[part, i, pl.ds(pl.multiple_of(start, piece), piece), pl.ds(block, 128)] = tile[at : at + piece]


def whole(count):
    return [pl.BlockSpec(memory_space=pltpu.VMEM)] * count


def on_device(chan, blk, voltages, fir_taps):
    frames = voltages.shape[1] // L
    parts, half = chan * blk, blk // 2
    feeds = blk * 8
    per, width = N1 // blk, HALF // chan
    chunks = min(per, 2)
    held = per // chunks
    twiddle, table = tables()
    dma = pltpu.SemaphoreType.DMA
    any_place = pl.BlockSpec(memory_space=pl.ANY)
    near = (per, half, width * 12, 2 * feeds)
    far = (per, half, width * 4, 2 * feeds)
    mine = pl.pallas_call(
        functools.partial(exchange_kernel, (frames, chan, blk)),
        out_shape=[jax.ShapeDtypeStruct(near, jnp.bfloat16), jax.ShapeDtypeStruct(far, jnp.bfloat16)],
        in_specs=whole(4),
        out_specs=[any_place, any_place],
        scratch_shapes=[
            pltpu.VMEM((8, (TAPS - 1) * L), jnp.bfloat16),
            pltpu.VMEM((frames * N1, 8, N2), jnp.float32),
            pltpu.VMEM((2 * N1, 4 * frames, 2 * N2), jnp.float32),
            pltpu.VMEM((1, parts, per * width, 128), jnp.bfloat16),
            pltpu.VMEM((chunks, parts, held * width, 128), jnp.bfloat16),
            pltpu.VMEM((1, parts, per * width, 128), jnp.bfloat16),
            pltpu.VMEM((chunks, parts, held * width, 128), jnp.bfloat16),
            pltpu.VMEM((1, parts // 2, per * width, 128), jnp.bfloat16),
            pltpu.VMEM((chunks, parts // 2, held * width, 128), jnp.bfloat16),
            pltpu.VMEM((feeds * width, 128), jnp.float32),
            pltpu.VMEM((feeds // 2 * width, 128), jnp.float32),
            pltpu.VMEM(near, jnp.bfloat16),
            pltpu.VMEM(far, jnp.bfloat16),
            dma((2,)),
            dma((2, 1 + chunks)),
            dma((2, 1 + chunks)),
            dma((2, per)),
            dma((2,)),
        ],
        compiler_params=pltpu.CompilerParams(vmem_limit_bytes=VMEM, collective_id=0, has_side_effects=True),
        name="exchange",
    )(voltages, fir_taps, jnp.asarray(twiddle), jnp.asarray(table))
    return pl.pallas_call(
        functools.partial(finish_kernel, blk, per, width, feeds),
        out_shape=jax.ShapeDtypeStruct((2, 8, feeds, width * N1), jnp.float32),
        in_specs=whole(2),
        out_specs=whole(1)[0],
        scratch_shapes=[pltpu.VMEM((feeds // 64, width * N1 * 8, 128), jnp.float32)],
        compiler_params=pltpu.CompilerParams(vmem_limit_bytes=VMEM),
        name="finish",
    )(*mine)


def solution(mesh):
    chan, blk = mesh.shape["chan"], mesh.shape["blk"]
    return jax.shard_map(
        functools.partial(on_device, chan, blk),
        mesh=mesh,
        in_specs=(P("blk", "chan"), P()),
        out_specs=P(None, "blk", None, "chan"),
        check_vma=False,
    )
```

```python
import functools
import math

import jax
import jax.numpy as jnp
import numpy as np
from jax import lax
from jax.experimental import pallas as pl
from jax.experimental.pallas import tpu as pltpu
from jax.sharding import PartitionSpec as P

TAPS = 8
L = 4096
C = 2048
N2 = 128
N1 = L // N2
HALF = C // N1
VMEM = 56 * 1024 * 1024


def tables():
    n2 = np.arange(N2)
    angle = 2.0 * np.pi * (np.arange(N1)[:, None] * n2[None, :] % L) / L
    twiddle = np.stack([np.cos(angle), np.sin(angle)]).astype(np.float32)
    angle = 2.0 * np.pi * (np.arange(HALF)[:, None] * n2[None, :] % N2) / N2
    cos, sin = np.cos(angle) / math.sqrt(L), np.sin(angle) / math.sqrt(L)
    matrix = np.block([[cos, sin], [-sin, cos]])
    high = matrix.astype(jnp.bfloat16)
    low = (matrix - high.astype(np.float64)).astype(jnp.bfloat16)
    return twiddle, np.concatenate([low, high])


def times(scale, value):
    return None if value is None else scale * value


def plus(a, b):
    return b if a is None else a if b is None else a + b


def minus(a, b):
    return a if b is None else -b if a is None else a - b


def real_dft(values):
    n = len(values)
    if n == 1:
        return [(values[0], None)]
    half = n // 2
    even, odd = real_dft(values[0::2]), real_dft(values[1::2])
    result = [None] * (half + 1)
    for k in range(half // 2 + 1):
        (er, ei), (odr, odi) = even[k], odd[k]
        if k == 0:
            tr, ti = odr, odi
        elif 4 * k == n:
            tr, ti = odi, -odr
        else:
            c, s = math.cos(2 * math.pi * k / n), math.sin(2 * math.pi * k / n)
            tr = plus(times(c, odr), times(s, odi))
            ti = minus(times(c, odi), times(s, odr))
        result[half - k] = (minus(er, tr), minus(ti, ei))
        result[k] = (plus(er, tr), plus(ei, ti))
    return result


def fir_stage(volt, halo, taps, filtered, frames):
    first, end = frames

    @pl.loop(0, N1)
    def _(n1):
        lane = pl.multiple_of(n1 * N2, N2)
        weights = [jnp.broadcast_to(taps[t : t + 1, pl.ds(lane, N2)], (8, N2)) for t in range(TAPS)]

        def frame(f):
            if f < 0:
                return halo[:, pl.ds((f + TAPS - 1) * L + lane, N2)].astype(jnp.float32)
            return volt[:, pl.ds(f * L + lane, N2)].astype(jnp.float32)

        window = [frame(f) for f in range(first - TAPS + 1, first)]
        for f in range(end - first):
            window.append(frame(first + f))
            total = weights[0] * window[f]
            for t in range(1, TAPS):
                total = total + weights[t] * window[f + t]
            filtered[(first + f) * N1 + n1] = total


def first_stage(filtered, twiddle, turned, part, frames):
    @pl.loop(0, frames)
    def _(f):
        spectrum = real_dft([filtered[(part * frames + f) * N1 + n1] for n1 in range(N1)])
        rows = pl.ds(pl.multiple_of(f * 8, 8), 8)
        for k1 in range(N1):
            if 2 * k1 <= N1:
                zr, zi = spectrum[k1]
            else:
                zr, zi = spectrum[N1 - k1]
                zi = -zi
            c = twiddle[0, k1 : k1 + 1, :]
            s = twiddle[1, k1 : k1 + 1, :]
            if k1 == 0:
                re, im = zr, jnp.zeros_like(zr)
            elif zi is None:
                re, im = c * zr, -(s * zr)
            else:
                re, im = c * zr + s * zi, c * zi - s * zr
            turned[part * N1 + k1, rows, pl.ds(0, N2)] = re
            turned[part * N1 + k1, rows, pl.ds(N2, N2)] = im


def second_stage(turned, first, second, table):
    contract = (((1,), (1,)), ((), ()))
    z = jnp.concatenate([turned[first], turned[second]], axis=0)
    zh = z.astype(jnp.bfloat16)
    zl = (z - zh.astype(jnp.float32)).astype(jnp.bfloat16)
    both = lax.dot_general(table[...], zh, contract, preferred_element_type=jnp.float32)
    rest = lax.dot_general(table[2 * HALF :], zl, contract, preferred_element_type=jnp.float32)
    out = both[2 * HALF :] + (both[: 2 * HALF] + rest)
    return [value.astype(jnp.bfloat16) for value in swap_halves(out[:HALF], out[HALF:])]


def regroup(groups, lane):
    count = len(groups)
    d = 1
    while d < count:
        low_side = (lane & d) == 0
        result = list(groups)
        for g in range(count):
            if g & d == 0:
                a, b = groups[g], groups[g | d]
                result[g] = jnp.where(low_side, a, pltpu.roll(b, d, 1))
                result[g | d] = jnp.where(low_side, pltpu.roll(a, 128 - d, 1), b)
        groups = result
        d *= 2
    return groups


def gather_feeds(get, blk, chan, width, place, grouped):
    lane = lax.broadcasted_iota(jnp.int32, (width, 128), 1)

    @pl.loop(0, blk, unroll=blk <= 8)
    def _(b):
        arrays = [get(c, b, part).astype(jnp.float32) for part in range(2) for c in range(chan)]
        for feed, value in enumerate(regroup(arrays, lane)):
            row = pl.multiple_of((place(b) * 8 + feed) * width, width)
            grouped[pl.ds(row, width), :] = value


def sides(grouped, ch, feeds, width):
    lane = lax.broadcasted_iota(jnp.int32, (feeds, 128), 1)
    value = grouped[pl.ds(ch, feeds, stride=width), :]
    other = pltpu.roll(value, 64, 1)
    other = jnp.where(lane < 64, -other, other)
    return value.astype(jnp.bfloat16), other.astype(jnp.bfloat16)


def product(left, right):
    return lax.dot_general(left, right, (((1,), (1,)), ((), ())), preferred_element_type=jnp.float32)


def paired(lefts, rights, order):
    rows = []
    for part in range(2):
        for one in order:
            zero = jnp.zeros_like(rights[one][part])
            rows.append(jnp.concatenate([rights[0][part] if one == 0 else zero, rights[1][part] if one else zero], axis=1))
    return product(jnp.concatenate(lefts, axis=1), jnp.concatenate(rows, axis=0))


def quad_by_channel(grouped, nearby, quad, feeds, width):
    near_feeds = feeds // 2
    full_rows, far_rows, own_rows = [], [], []
    for pair in range(2):
        lefts, rights, own_lefts, own_rights, full = [], [], [], [], []
        for one in range(2):
            ch = quad * 4 + pair * 2 + one
            value, other = sides(grouped, ch, feeds, width)
            full.append(product(value[:near_feeds], jnp.concatenate([value, other], axis=0)))
            lefts.append(value[near_feeds:])
            rights.append((value[:near_feeds], other[:near_feeds]))
            value, other = sides(nearby, ch, near_feeds, width)
            own_lefts.append(value)
            own_rights.append((value, other))
        full_rows.append(full)
        far_rows.append(paired(lefts, rights, (1, 0)))
        own_rows.append(paired(own_lefts, own_rights, (0, 1)))
    return full_rows, far_rows, own_rows


def square(value):
    turned = value.T
    other = jnp.concatenate([-turned[64:], turned[:64]], axis=0)
    right = jnp.concatenate([turned, other], axis=1).astype(jnp.bfloat16)
    out = jnp.dot(value.astype(jnp.bfloat16), right, preferred_element_type=jnp.float32)
    return out[:, :128], out[:, 128:]


def quad_of_64(grouped, nearby, quad, width):
    lane = lax.broadcasted_iota(jnp.int32, (32, 128), 1)
    low, first, third = lane < 64, lane < 32, lane < 96

    def roll(value, shift):
        return pltpu.roll(value, shift, 1)

    full_rows, far_rows = [], []
    for pair in range(2):
        ch = quad * 4 + pair * 2
        value = jnp.concatenate([grouped[pl.ds(ch + one, 64, stride=width), :] for one in range(2)], axis=0)
        re, im = square(value)
        full_rows.append(
            [
                jnp.where(low, re[:32], roll(im[:32], 64)),
                jnp.where(low, roll(re[64:96], 64), im[64:96]),
            ]
        )
        far_rows.append(
            jnp.where(
                low,
                jnp.where(first, roll(re[96:], 64), roll(re[32:64], 32)),
                jnp.where(third, im[96:], roll(im[32:64], 96)),
            )
        )
    value = jnp.concatenate([nearby[pl.ds(quad * 4 + one, 32, stride=width), :] for one in range(4)], axis=0)
    re, im = square(value)
    own_rows = [
        jnp.where(low, jnp.where(first, re[:32], re[32:64]), roll(jnp.where(first, im[:32], im[32:64]), 64)),
        jnp.where(low, roll(jnp.where(third, re[64:96], re[96:]), 64), jnp.where(third, im[64:96], im[96:])),
    ]
    return full_rows, far_rows, own_rows


def correlate(grouped, nearby, half, width, spectra_count, near, far):
    feeds = 16 * half
    scale = 1.0 / spectra_count

    @pl.loop(0, width // 4, unroll=True)
    def _(quad):
        if feeds == 64:
            full_rows, far_rows, own_rows = quad_of_64(grouped, nearby, quad, width)
        else:
            full_rows, far_rows, own_rows = quad_by_channel(grouped, nearby, quad, feeds, width)
        for b in range(half):
            cut = slice(b * 8, b * 8 + 8)

            def put(ref, row, first, second):
                rows = jnp.concatenate([first[cut], second[cut]], axis=0) * scale
                ref[b, pl.ds(pl.multiple_of(row, 16), 16), :] = rows.astype(jnp.bfloat16)

            for pair in range(2):
                put(near, (quad * 2 + pair) * 16, *full_rows[pair])
            put(near, width * 8 + quad * 16, *own_rows)
            put(far, quad * 16, *far_rows)


def exchange_kernel(
    sizes, volt, taps, twiddle, table, out_near, out_far,
    halo, filtered, turned, sent_late, sent, seen_late, seen, near_late, seen_near, grouped, nearby, near, far,
    halo_sems, send_sems, seen_sems, product_sems, out_sems,
):
    frames, chan, blk = sizes
    parts, half = chan * blk, blk // 2
    width = HALF // chan
    per = N1 // blk
    chunks, held = sent.shape[0], per // sent.shape[0]
    c, b = lax.axis_index("chan"), lax.axis_index("blk")
    side, spot = lax.div(b, half), lax.rem(b, half)
    barrier = pltpu.get_barrier_semaphore()

    def remote(src, dst, send_sem, recv_sem, to_c, to_b):
        return pltpu.make_async_remote_copy(
            src_ref=src,
            dst_ref=dst,
            send_sem=send_sem,
            recv_sem=recv_sem,
            device_id={"chan": to_c, "blk": to_b},
            device_id_type=pl.DeviceIdType.MESH,
        )

    @pl.loop(1, parts)
    def _(d):
        other = lax.rem(c * blk + b + d, parts)
        pl.semaphore_signal(
            barrier,
            inc=1,
            device_id={"chan": lax.div(other, blk), "blk": lax.rem(other, blk)},
            device_id_type=pl.DeviceIdType.MESH,
        )

    @pl.when(c == 0)
    def _():
        halo[...] = jnp.zeros_like(halo)

    def send(part, q, slot, held, sent, seen, seen_near):
        @pl.loop(0, half)
        def _(t):
            at = lax.rem(spot + 1 + t, half)
            near_b, far_b = side * half + at, (1 - side) * half + at
            for to_b in (far_b, near_b):
                base = part * N1 + to_b * per + q * held
                for first in range(0, held, 2):
                    second = min(first + 1, held - 1)
                    values = second_stage(turned, base + first, base + second, table)
                    for kk in range(first, second + 1):
                        for to_c in range(chan):
                            rows = pl.ds(kk * width, width)
                            sent[q, to_c * blk + to_b, rows, :] = values[kk - first][to_c * width : (to_c + 1) * width]
                if to_b is far_b:
                    for u in range(chan):
                        to_c = lax.rem(c + u, chan)
                        block = sent.at[q, to_c * blk + far_b]
                        dst = seen.at[q, c * blk + b]
                        remote(block, dst, send_sems.at[0, slot], seen_sems.at[0, slot], to_c, far_b).start()
            for u in range(chan):
                to_c = lax.rem(c + u, chan)
                for kind, to_b, dst in (
                    (0, near_b, seen.at[q, c * blk + b]),
                    (1, far_b, seen_near.at[q, c * half + spot]),
                ):
                    block = sent.at[q, to_c * blk + to_b]
                    copy = remote(block, dst, send_sems.at[kind, slot], seen_sems.at[kind, slot], to_c, near_b)
                    if u == 0:
                        pl.when(near_b != b)(copy.start)
                        pl.when(near_b == b)(pltpu.make_async_copy(block, dst, seen_sems.at[kind, slot]).start)
                    else:
                        copy.start()

    count = frames // 2
    fir_stage(volt, halo, taps, filtered, (count, frames))
    pl.semaphore_wait(barrier, parts - 1)
    last = volt.at[:, pl.ds((frames - TAPS + 1) * L, (TAPS - 1) * L)]
    halo_copy = remote(last, halo, halo_sems.at[0], halo_sems.at[1], lax.rem(c + 1, chan), b)

    @pl.when(c < chan - 1)
    def _():
        halo_copy.start()

    first_stage(filtered, twiddle, turned, 1, count)
    send(1, 0, 0, per, sent_late, seen_late, near_late)

    @pl.when(c > 0)
    def _():
        halo_copy.wait_recv()

    fir_stage(volt, halo, taps, filtered, (0, count))
    first_stage(filtered, twiddle, turned, 0, count)
    for q in range(chunks):
        send(0, q, 1 + q, held, sent, seen, seen_near)

    def arrived(ref, kind, q, slot):
        pltpu.make_async_copy(ref.at[q], ref.at[q], seen_sems.at[kind, slot]).wait()

    arrived(seen_late, 0, 0, 0)
    arrived(near_late, 1, 0, 0)
    for q in range(chunks):
        arrived(seen, 0, q, 1 + q)
        arrived(seen_near, 1, q, 1 + q)
        for kk in range(held):
            index = q * held + kk

            def block(late, early, source, part):
                if part == 1:
                    return late[0, source, pl.ds(index * width, width), :]
                return early[q, source, pl.ds(kk * width, width), :]

            def get(from_c, from_b, part):
                return block(seen_late, seen, from_c * blk + from_b, part)

            def get_near(from_c, at, part):
                return block(near_late, seen_near, from_c * half + at, part)

            gather_feeds(get, blk, chan, width, lambda from_b: lax.rem(from_b + side * half, blk), grouped)
            gather_feeds(get_near, half, chan, width, lambda at: at, nearby)
            correlate(grouped, nearby, half, width, frames * chan, near.at[index], far.at[index])

            @pl.loop(0, half)
            def _(t):
                at = lax.rem(spot + 1 + t, half)
                near_b, far_b = side * half + at, (1 - side) * half + at
                remote(
                    far.at[index, at], out_far.at[index, spot], product_sems.at[1, index], out_sems.at[1], c, far_b
                ).start()
                copy = remote(
                    near.at[index, at], out_near.at[index, spot], product_sems.at[0, index], out_sems.at[0], c, near_b
                )
                pl.when(at != spot)(copy.start)

            pltpu.make_async_copy(near.at[index, spot], out_near.at[index, spot], out_sems.at[0]).start()

    pltpu.make_async_copy(out_near, out_near, out_sems.at[0]).wait()
    pltpu.make_async_copy(out_far, out_far, out_sems.at[1]).wait()
    for slot in range(1 + chunks):
        ref, q = (sent_late, 0) if slot == 0 else (sent, slot - 1)
        for kind, number in enumerate((parts, chan * half)):
            piece = ref.at[q, pl.ds(0, number - 1)]
            pltpu.make_async_copy(piece, piece, send_sems.at[kind, slot]).wait()
    for index in range(per):
        piece = near.at[index, pl.ds(0, half - 1)]
        pltpu.make_async_copy(piece, piece, product_sems.at[0, index]).wait()
        pltpu.make_async_copy(far.at[index], far.at[index], product_sems.at[1, index]).wait()

    @pl.when(c < chan - 1)
    def _():
        halo_copy.wait_send()


def swap_halves(first, second):
    low_side = lax.broadcasted_iota(jnp.int32, first.shape, 1) < 64
    return [
        jnp.where(low_side, first, pltpu.roll(second, 64, 1)),
        jnp.where(low_side, pltpu.roll(first, 64, 1), second),
    ]


def join(own, other, feeds):
    count = feeds // 2
    if count % 128 == 0:
        cuts = [slice(at, at + count) for at in range(0, 2 * feeds, count)]
        return [
            jnp.concatenate([own[:, cuts[0]], other[:, cuts[1]], own[:, cuts[2]], other[:, cuts[3]]], axis=1),
            jnp.concatenate([own[:, cuts[1]], other[:, cuts[0]], own[:, cuts[3]], other[:, cuts[2]]], axis=1),
        ]
    even = lax.broadcasted_iota(jnp.int32, own.shape, 1) // count % 2 == 0
    return [
        jnp.where(even, own, other),
        jnp.where(even, pltpu.roll(own, 2 * feeds - count, 1), pltpu.roll(other, count, 1)),
    ]


def finish_kernel(blk, per, width, feeds, near, far, out, wide):
    half = blk // 2
    side = lax.div(lax.axis_index("blk"), half)

    def put(k2, k1, rows):
        row = pl.multiple_of((k2 * N1 + k1) * 8, 8)
        for first in range(0, 2 * feeds, 128):
            wide[first // 128, pl.ds(row, 8), :] = rows[:, first : first + 128]

    @pl.loop(0, half)
    def _(at):
        near_b, far_b = side * half + at, (1 - side) * half + at
        for kk in range(per):
            value = near[kk, at].astype(jnp.float32)
            other = far[kk, at].astype(jnp.float32)
            for k2 in range(width):
                put(k2, near_b * per + kk, value[k2 * 8 : k2 * 8 + 8])
            for pair in range(width // 2):
                own = value[(width + pair) * 8 : (width + pair) * 8 + 8]
                for one, rows in enumerate(join(own, other[pair * 8 : pair * 8 + 8], feeds)):
                    put(2 * pair + one, far_b * per + kk, rows)

    count = feeds // 2
    piece = min(count, 128)
    for i in range(8):
        for block in range(0, width * N1, 128):
            for first in range(0, 2 * feeds, 128):
                tile = wide[first // 128, pl.ds(block * 8 + i, 128, stride=8), :].T
                for at in range(0, 128, piece):
                    part, rest = divmod(first + at, feeds)
                    which, j = divmod(rest, count)
                    start = (side if which == 0 else 1 - side) * count + j
                    out[part, i, pl.ds(pl.multiple_of(start, piece), piece), pl.ds(block, 128)] = tile[at : at + piece]


def whole(count):
    return [pl.BlockSpec(memory_space=pltpu.VMEM)] * count


def on_device(chan, blk, voltages, fir_taps):
    frames = voltages.shape[1] // L
    parts, half = chan * blk, blk // 2
    feeds = blk * 8
    per, width = N1 // blk, HALF // chan
    chunks = min(per, 2)
    held = per // chunks
    twiddle, table = tables()
    dma = pltpu.SemaphoreType.DMA
    any_place = pl.BlockSpec(memory_space=pl.ANY)
    near = (per, half, width * 12, 2 * feeds)
    far = (per, half, width * 4, 2 * feeds)
    mine = pl.pallas_call(
        functools.partial(exchange_kernel, (frames, chan, blk)),
        out_shape=[jax.ShapeDtypeStruct(near, jnp.bfloat16), jax.ShapeDtypeStruct(far, jnp.bfloat16)],
        in_specs=whole(4),
        out_specs=[any_place, any_place],
        scratch_shapes=[
            pltpu.VMEM((8, (TAPS - 1) * L), jnp.bfloat16),
            pltpu.VMEM((frames * N1, 8, N2), jnp.float32),
            pltpu.VMEM((2 * N1, 4 * frames, 2 * N2), jnp.float32),
            pltpu.VMEM((1, parts, per * width, 128), jnp.bfloat16),
            pltpu.VMEM((chunks, parts, held * width, 128), jnp.bfloat16),
            pltpu.VMEM((1, parts, per * width, 128), jnp.bfloat16),
            pltpu.VMEM((chunks, parts, held * width, 128), jnp.bfloat16),
            pltpu.VMEM((1, parts // 2, per * width, 128), jnp.bfloat16),
            pltpu.VMEM((chunks, parts // 2, held * width, 128), jnp.bfloat16),
            pltpu.VMEM((feeds * width, 128), jnp.float32),
            pltpu.VMEM((feeds // 2 * width, 128), jnp.float32),
            pltpu.VMEM(near, jnp.bfloat16),
            pltpu.VMEM(far, jnp.bfloat16),
            dma((2,)),
            dma((2, 1 + chunks)),
            dma((2, 1 + chunks)),
            dma((2, per)),
            dma((2,)),
        ],
        compiler_params=pltpu.CompilerParams(vmem_limit_bytes=VMEM, collective_id=0, has_side_effects=True),
        name="exchange",
    )(voltages, fir_taps, jnp.asarray(twiddle), jnp.asarray(table))
    return pl.pallas_call(
        functools.partial(finish_kernel, blk, per, width, feeds),
        out_shape=jax.ShapeDtypeStruct((2, 8, feeds, width * N1), jnp.float32),
        in_specs=whole(2),
        out_specs=whole(1)[0],
        scratch_shapes=[pltpu.VMEM((feeds // 64, width * N1 * 8, 128), jnp.float32)],
        compiler_params=pltpu.CompilerParams(vmem_limit_bytes=VMEM),
        name="finish",
    )(*mine)


def solution(mesh):
    chan, blk = mesh.shape["chan"], mesh.shape["blk"]
    return jax.shard_map(
        functools.partial(on_device, chan, blk),
        mesh=mesh,
        in_specs=(P("blk", "chan"), P()),
        out_specs=P(None, "blk", None, "chan"),
        check_vma=False,
    )
```

```python
import functools
import math

import jax
import jax.numpy as jnp
import numpy as np
from jax import lax
from jax.experimental import pallas as pl
from jax.experimental.pallas import tpu as pltpu
from jax.sharding import PartitionSpec as P

TAPS = 8
L = 4096
C = 2048
N2 = 128
N1 = L // N2
HALF = C // N1
VMEM = 56 * 1024 * 1024


def tables():
    n2 = np.arange(N2)
    angle = 2.0 * np.pi * (np.arange(N1)[:, None] * n2[None, :] % L) / L
    twiddle = np.stack([np.cos(angle), np.sin(angle)]).astype(np.float32)
    angle = 2.0 * np.pi * (np.arange(HALF)[:, None] * n2[None, :] % N2) / N2
    cos, sin = np.cos(angle) / math.sqrt(L), np.sin(angle) / math.sqrt(L)
    matrix = np.block([[cos, sin], [-sin, cos]])
    high = matrix.astype(jnp.bfloat16)
    low = (matrix - high.astype(np.float64)).astype(jnp.bfloat16)
    return twiddle, np.concatenate([low, high])


def times(scale, value):
    return None if value is None else scale * value


def plus(a, b):
    return b if a is None else a if b is None else a + b


def minus(a, b):
    return a if b is None else -b if a is None else a - b


def real_dft(values):
    n = len(values)
    if n == 1:
        return [(values[0], None)]
    half = n // 2
    even, odd = real_dft(values[0::2]), real_dft(values[1::2])
    result = [None] * (half + 1)
    for k in range(half // 2 + 1):
        (er, ei), (odr, odi) = even[k], odd[k]
        if k == 0:
            tr, ti = odr, odi
        elif 4 * k == n:
            tr, ti = odi, -odr
        else:
            c, s = math.cos(2 * math.pi * k / n), math.sin(2 * math.pi * k / n)
            tr = plus(times(c, odr), times(s, odi))
            ti = minus(times(c, odi), times(s, odr))
        result[half - k] = (minus(er, tr), minus(ti, ei))
        result[k] = (plus(er, tr), plus(ei, ti))
    return result


def fir_stage(volt, halo, taps, filtered, frames):
    first, end = frames

    @pl.loop(0, N1)
    def _(n1):
        lane = pl.multiple_of(n1 * N2, N2)
        weights = [jnp.broadcast_to(taps[t : t + 1, pl.ds(lane, N2)], (8, N2)) for t in range(TAPS)]

        def frame(f):
            if f < 0:
                return halo[:, pl.ds((f + TAPS - 1) * L + lane, N2)].astype(jnp.float32)
            return volt[:, pl.ds(f * L + lane, N2)].astype(jnp.float32)

        window = [frame(f) for f in range(first - TAPS + 1, first)]
        for f in range(end - first):
            window.append(frame(first + f))
            total = weights[0] * window[f]
            for t in range(1, TAPS):
                total = total + weights[t] * window[f + t]
            filtered[(first + f) * N1 + n1] = total


def first_stage(filtered, twiddle, turned, part, frames):
    @pl.loop(0, frames)
    def _(f):
        spectrum = real_dft([filtered[(part * frames + f) * N1 + n1] for n1 in range(N1)])
        rows = pl.ds(pl.multiple_of(f * 8, 8), 8)
        for k1 in range(N1):
            if 2 * k1 <= N1:
                zr, zi = spectrum[k1]
            else:
                zr, zi = spectrum[N1 - k1]
                zi = -zi
            c = twiddle[0, k1 : k1 + 1, :]
            s = twiddle[1, k1 : k1 + 1, :]
            if k1 == 0:
                re, im = zr, jnp.zeros_like(zr)
            elif zi is None:
                re, im = c * zr, -(s * zr)
            else:
                re, im = c * zr + s * zi, c * zi - s * zr
            turned[part * N1 + k1, rows, pl.ds(0, N2)] = re
            turned[part * N1 + k1, rows, pl.ds(N2, N2)] = im


def second_stage(turned, first, second, table):
    contract = (((1,), (1,)), ((), ()))
    z = jnp.concatenate([turned[first], turned[second]], axis=0)
    zh = z.astype(jnp.bfloat16)
    zl = (z - zh.astype(jnp.float32)).astype(jnp.bfloat16)
    both = lax.dot_general(table[...], zh, contract, preferred_element_type=jnp.float32)
    rest = lax.dot_general(table[2 * HALF :], zl, contract, preferred_element_type=jnp.float32)
    out = both[2 * HALF :] + (both[: 2 * HALF] + rest)
    return [value.astype(jnp.bfloat16) for value in swap_halves(out[:HALF], out[HALF:])]


def regroup(groups, lane):
    count = len(groups)
    d = 1
    while d < count:
        low_side = (lane & d) == 0
        result = list(groups)
        for g in range(count):
            if g & d == 0:
                a, b = groups[g], groups[g | d]
                result[g] = jnp.where(low_side, a, pltpu.roll(b, d, 1))
                result[g | d] = jnp.where(low_side, pltpu.roll(a, 128 - d, 1), b)
        groups = result
        d *= 2
    return groups


def gather_feeds(get, count, chan, width, start, grouped):
    lane = lax.broadcasted_iota(jnp.int32, (width, 128), 1)

    @pl.loop(0, count, unroll=count <= 8)
    def _(at):
        arrays = [get(c, at, part).astype(jnp.float32) for part in range(2) for c in range(chan)]
        for feed, value in enumerate(regroup(arrays, lane)):
            row = pl.multiple_of(((start + at) * 8 + feed) * width, width)
            grouped[pl.ds(row, width), :] = value


def sides(grouped, ch, feeds, width):
    lane = lax.broadcasted_iota(jnp.int32, (feeds, 128), 1)
    value = grouped[pl.ds(ch, feeds, stride=width), :]
    other = pltpu.roll(value, 64, 1)
    other = jnp.where(lane < 64, -other, other)
    return value.astype(jnp.bfloat16), other.astype(jnp.bfloat16)


def product(left, right):
    return lax.dot_general(left, right, (((1,), (1,)), ((), ())), preferred_element_type=jnp.float32)


def paired(lefts, rights, order):
    rows = []
    for part in range(2):
        for one in order:
            zero = jnp.zeros_like(rights[one][part])
            rows.append(jnp.concatenate([rights[0][part] if one == 0 else zero, rights[1][part] if one else zero], axis=1))
    return product(jnp.concatenate(lefts, axis=1), jnp.concatenate(rows, axis=0))


def quad_by_channel(grouped, nearby, quad, feeds, width):
    near_feeds = feeds // 2
    full_rows, far_rows, own_rows = [], [], []
    for pair in range(2):
        lefts, rights, own_lefts, own_rights, full = [], [], [], [], []
        for one in range(2):
            ch = quad * 4 + pair * 2 + one
            value, other = sides(grouped, ch, feeds, width)
            full.append(product(value[:near_feeds], jnp.concatenate([value, other], axis=0)))
            lefts.append(value[near_feeds:])
            rights.append((value[:near_feeds], other[:near_feeds]))
            value, other = sides(nearby, ch, near_feeds, width)
            own_lefts.append(value)
            own_rights.append((value, other))
        full_rows.append(full)
        far_rows.append(paired(lefts, rights, (1, 0)))
        own_rows.append(paired(own_lefts, own_rights, (0, 1)))
    return full_rows, far_rows, own_rows


def square(value):
    turned = value.T
    other = jnp.concatenate([-turned[64:], turned[:64]], axis=0)
    right = jnp.concatenate([turned, other], axis=1).astype(jnp.bfloat16)
    out = jnp.dot(value.astype(jnp.bfloat16), right, preferred_element_type=jnp.float32)
    return out[:, :128], out[:, 128:]


def quad_of_64(grouped, nearby, quad, width):
    lane = lax.broadcasted_iota(jnp.int32, (32, 128), 1)
    low, first, third = lane < 64, lane < 32, lane < 96

    def roll(value, shift):
        return pltpu.roll(value, shift, 1)

    full_rows, far_rows = [], []
    for pair in range(2):
        ch = quad * 4 + pair * 2
        value = jnp.concatenate([grouped[pl.ds(ch + one, 64, stride=width), :] for one in range(2)], axis=0)
        re, im = square(value)
        full_rows.append(
            [
                jnp.where(low, re[:32], roll(im[:32], 64)),
                jnp.where(low, roll(re[64:96], 64), im[64:96]),
            ]
        )
        far_rows.append(
            jnp.where(
                low,
                jnp.where(first, roll(re[96:], 64), roll(re[32:64], 32)),
                jnp.where(third, im[96:], roll(im[32:64], 96)),
            )
        )
    value = jnp.concatenate([nearby[pl.ds(quad * 4 + one, 32, stride=width), :] for one in range(4)], axis=0)
    re, im = square(value)
    own_rows = [
        jnp.where(low, jnp.where(first, re[:32], re[32:64]), roll(jnp.where(first, im[:32], im[32:64]), 64)),
        jnp.where(low, roll(jnp.where(third, re[64:96], re[96:]), 64), jnp.where(third, im[64:96], im[96:])),
    ]
    return full_rows, far_rows, own_rows


def correlate(grouped, nearby, half, width, spectra_count, near, far):
    feeds = 16 * half
    scale = 1.0 / spectra_count

    @pl.loop(0, width // 4, unroll=True)
    def _(quad):
        if feeds == 64:
            full_rows, far_rows, own_rows = quad_of_64(grouped, nearby, quad, width)
        else:
            full_rows, far_rows, own_rows = quad_by_channel(grouped, nearby, quad, feeds, width)
        for b in range(half):
            cut = slice(b * 8, b * 8 + 8)

            def put(ref, row, first, second):
                rows = jnp.concatenate([first[cut], second[cut]], axis=0) * scale
                ref[b, pl.ds(pl.multiple_of(row, 16), 16), :] = rows.astype(jnp.bfloat16)

            for pair in range(2):
                put(near, (quad * 2 + pair) * 16, *full_rows[pair])
            put(near, width * 8 + quad * 16, *own_rows)
            put(far, quad * 16, *far_rows)


def exchange_kernel(
    sizes, volt, taps, twiddle, table, out_near, out_far,
    halo, filtered, turned, to_far_late, to_far, to_near_late, to_near,
    from_far_late, from_far, from_near_late, from_near, grouped, nearby, near, far,
    halo_sems, send_sems, seen_sems, product_sems, out_sems,
):
    frames, chan, blk = sizes
    parts, half = chan * blk, blk // 2
    width = HALF // chan
    per = N1 // blk
    chunks, held = to_far.shape[0], per // to_far.shape[0]
    c, b = lax.axis_index("chan"), lax.axis_index("blk")
    side, spot = lax.div(b, half), lax.rem(b, half)
    barrier = pltpu.get_barrier_semaphore()

    def remote(src, dst, send_sem, recv_sem, to_c, to_b):
        return pltpu.make_async_remote_copy(
            src_ref=src,
            dst_ref=dst,
            send_sem=send_sem,
            recv_sem=recv_sem,
            device_id={"chan": to_c, "blk": to_b},
            device_id_type=pl.DeviceIdType.MESH,
        )

    @pl.loop(1, parts)
    def _(d):
        other = lax.rem(c * blk + b + d, parts)
        pl.semaphore_signal(
            barrier,
            inc=1,
            device_id={"chan": lax.div(other, blk), "blk": lax.rem(other, blk)},
            device_id_type=pl.DeviceIdType.MESH,
        )

    @pl.when(c == 0)
    def _():
        halo[...] = jnp.zeros_like(halo)

    def send(part, q, slot, held, to_far, to_near, from_far, from_near):
        rows = held * width

        @pl.loop(0, half)
        def _(t):
            at = lax.rem(spot + 1 + t, half)
            near_b, far_b = side * half + at, (1 - side) * half + at
            for to_b, refs in ((far_b, ((to_far, 0), (to_near, rows))), (near_b, ((to_near, 0),))):
                base = part * N1 + to_b * per + q * held
                for first in range(0, held, 2):
                    second = min(first + 1, held - 1)
                    values = second_stage(turned, base + first, base + second, table)
                    for kk in range(first, second + 1):
                        for to_c in range(chan):
                            value = values[kk - first][to_c * width : (to_c + 1) * width]
                            for ref, start in refs:
                                ref[q, to_c * half + at, pl.ds(start + kk * width, width), :] = value
                if to_b is far_b:
                    for u in range(chan):
                        to_c = lax.rem(c + u, chan)
                        block = to_far.at[q, to_c * half + at]
                        dst = from_far.at[q, c * half + spot]
                        remote(block, dst, send_sems.at[0, slot], seen_sems.at[0, slot], to_c, far_b).start()
            for u in range(chan):
                to_c = lax.rem(c + u, chan)
                block, dst = to_near.at[q, to_c * half + at], from_near.at[q, c * half + spot]
                copy = remote(block, dst, send_sems.at[1, slot], seen_sems.at[1, slot], to_c, near_b)
                if u == 0:
                    pl.when(at != spot)(copy.start)
                    pl.when(at == spot)(pltpu.make_async_copy(block, dst, seen_sems.at[1, slot]).start)
                else:
                    copy.start()

    count = frames // 2
    fir_stage(volt, halo, taps, filtered, (count, frames))
    pl.semaphore_wait(barrier, parts - 1)
    last = volt.at[:, pl.ds((frames - TAPS + 1) * L, (TAPS - 1) * L)]
    halo_copy = remote(last, halo, halo_sems.at[0], halo_sems.at[1], lax.rem(c + 1, chan), b)

    @pl.when(c < chan - 1)
    def _():
        halo_copy.start()

    first_stage(filtered, twiddle, turned, 1, count)
    send(1, 0, 0, per, to_far_late, to_near_late, from_far_late, from_near_late)

    @pl.when(c > 0)
    def _():
        halo_copy.wait_recv()

    fir_stage(volt, halo, taps, filtered, (0, count))
    first_stage(filtered, twiddle, turned, 0, count)
    for q in range(chunks):
        send(0, q, 1 + q, held, to_far, to_near, from_far, from_near)

    def arrived(ref, kind, q, slot):
        pltpu.make_async_copy(ref.at[q], ref.at[q], seen_sems.at[kind, slot]).wait()

    arrived(from_far_late, 0, 0, 0)
    arrived(from_near_late, 1, 0, 0)
    for q in range(chunks):
        arrived(from_far, 0, q, 1 + q)
        arrived(from_near, 1, q, 1 + q)
        for kk in range(held):
            index = q * held + kk

            def reader(late, early, second):
                def get(from_c, at, part):
                    source = from_c * half + at
                    if part == 1:
                        return late[0, source, pl.ds((second * per + index) * width, width), :]
                    return early[q, source, pl.ds((second * held + kk) * width, width), :]

                return get

            gather_feeds(reader(from_near_late, from_near, 0), half, chan, width, 0, grouped)
            gather_feeds(reader(from_far_late, from_far, 0), half, chan, width, half, grouped)
            gather_feeds(reader(from_near_late, from_near, 1), half, chan, width, 0, nearby)
            correlate(grouped, nearby, half, width, frames * chan, near.at[index], far.at[index])

            @pl.loop(0, half)
            def _(t):
                at = lax.rem(spot + 1 + t, half)
                near_b, far_b = side * half + at, (1 - side) * half + at
                remote(
                    far.at[index, at], out_far.at[index, spot], product_sems.at[1, index], out_sems.at[1], c, far_b
                ).start()
                copy = remote(
                    near.at[index, at], out_near.at[index, spot], product_sems.at[0, index], out_sems.at[0], c, near_b
                )
                pl.when(at != spot)(copy.start)

            pltpu.make_async_copy(near.at[index, spot], out_near.at[index, spot], out_sems.at[0]).start()

    pltpu.make_async_copy(out_near, out_near, out_sems.at[0]).wait()
    pltpu.make_async_copy(out_far, out_far, out_sems.at[1]).wait()
    for slot in range(1 + chunks):
        q = max(slot - 1, 0)
        piece = (to_far if slot else to_far_late).at[q]
        pltpu.make_async_copy(piece, piece, send_sems.at[0, slot]).wait()
        piece = (to_near if slot else to_near_late).at[q, pl.ds(0, chan * half - 1)]
        pltpu.make_async_copy(piece, piece, send_sems.at[1, slot]).wait()
    for index in range(per):
        piece = near.at[index, pl.ds(0, half - 1)]
        pltpu.make_async_copy(piece, piece, product_sems.at[0, index]).wait()
        pltpu.make_async_copy(far.at[index], far.at[index], product_sems.at[1, index]).wait()

    @pl.when(c < chan - 1)
    def _():
        halo_copy.wait_send()


def swap_halves(first, second):
    low_side = lax.broadcasted_iota(jnp.int32, first.shape, 1) < 64
    return [
        jnp.where(low_side, first, pltpu.roll(second, 64, 1)),
        jnp.where(low_side, pltpu.roll(first, 64, 1), second),
    ]


def join(own, other, feeds):
    count = feeds // 2
    if count % 128 == 0:
        cuts = [slice(at, at + count) for at in range(0, 2 * feeds, count)]
        return [
            jnp.concatenate([own[:, cuts[0]], other[:, cuts[1]], own[:, cuts[2]], other[:, cuts[3]]], axis=1),
            jnp.concatenate([own[:, cuts[1]], other[:, cuts[0]], own[:, cuts[3]], other[:, cuts[2]]], axis=1),
        ]
    even = lax.broadcasted_iota(jnp.int32, own.shape, 1) // count % 2 == 0
    return [
        jnp.where(even, own, other),
        jnp.where(even, pltpu.roll(own, 2 * feeds - count, 1), pltpu.roll(other, count, 1)),
    ]


def finish_kernel(blk, per, width, feeds, near, far, out, wide):
    half = blk // 2
    side = lax.div(lax.axis_index("blk"), half)

    def put(k2, k1, rows):
        row = pl.multiple_of((k2 * N1 + k1) * 8, 8)
        for first in range(0, 2 * feeds, 128):
            wide[first // 128, pl.ds(row, 8), :] = rows[:, first : first + 128]

    i = pl.program_id(0)

    @pl.when(i == 0)
    def _():
        @pl.loop(0, half)
        def _(at):
            near_b, far_b = side * half + at, (1 - side) * half + at
            for kk in range(per):
                value = near[kk, at].astype(jnp.float32)
                other = far[kk, at].astype(jnp.float32)
                for k2 in range(width):
                    put(k2, near_b * per + kk, value[k2 * 8 : k2 * 8 + 8])
                for pair in range(width // 2):
                    own = value[(width + pair) * 8 : (width + pair) * 8 + 8]
                    for one, rows in enumerate(join(own, other[pair * 8 : pair * 8 + 8], feeds)):
                        put(2 * pair + one, far_b * per + kk, rows)

    count = feeds // 2
    piece = min(count, 128)
    for block in range(0, width * N1, 128):
        for first in range(0, 2 * feeds, 128):
            tile = wide[first // 128, pl.ds(block * 8 + i, 128, stride=8), :].T
            for at in range(0, 128, piece):
                part, rest = divmod(first + at, feeds)
                which, j = divmod(rest, count)
                start = (side if which == 0 else 1 - side) * count + j
                out[part, 0, pl.ds(pl.multiple_of(start, piece), piece), pl.ds(block, 128)] = tile[at : at + piece]


def whole(count):
    return [pl.BlockSpec(memory_space=pltpu.VMEM)] * count


def on_device(chan, blk, voltages, fir_taps):
    frames = voltages.shape[1] // L
    parts, half = chan * blk, blk // 2
    feeds = blk * 8
    per, width = N1 // blk, HALF // chan
    chunks = per
    twiddle, table = tables()
    dma = pltpu.SemaphoreType.DMA
    blocks = [
        pltpu.VMEM((pieces, parts // 2, sets * width * per // pieces, 128), jnp.bfloat16)
        for sets in (1, 2)
        for pieces in (1, chunks)
    ]
    any_place = pl.BlockSpec(memory_space=pl.ANY)
    near = (per, half, width * 12, 2 * feeds)
    far = (per, half, width * 4, 2 * feeds)
    mine = pl.pallas_call(
        functools.partial(exchange_kernel, (frames, chan, blk)),
        out_shape=[jax.ShapeDtypeStruct(near, jnp.bfloat16), jax.ShapeDtypeStruct(far, jnp.bfloat16)],
        in_specs=whole(4),
        out_specs=[any_place, any_place],
        scratch_shapes=[
            pltpu.VMEM((8, (TAPS - 1) * L), jnp.bfloat16),
            pltpu.VMEM((frames * N1, 8, N2), jnp.float32),
            pltpu.VMEM((2 * N1, 4 * frames, 2 * N2), jnp.float32),
            *blocks,
            *blocks,
            pltpu.VMEM((feeds * width, 128), jnp.float32),
            pltpu.VMEM((feeds // 2 * width, 128), jnp.float32),
            pltpu.VMEM(near, jnp.bfloat16),
            pltpu.VMEM(far, jnp.bfloat16),
            dma((2,)),
            dma((2, 1 + chunks)),
            dma((2, 1 + chunks)),
            dma((2, per)),
            dma((2,)),
        ],
        compiler_params=pltpu.CompilerParams(vmem_limit_bytes=VMEM, collective_id=0, has_side_effects=True),
        name="exchange",
    )(voltages, fir_taps, jnp.asarray(twiddle), jnp.asarray(table))
    return pl.pallas_call(
        functools.partial(finish_kernel, blk, per, width, feeds),
        out_shape=jax.ShapeDtypeStruct((2, 8, feeds, width * N1), jnp.float32),
        grid=(8,),
        in_specs=whole(2),
        out_specs=pl.BlockSpec((2, 1, feeds, width * N1), lambda i: (0, i, 0, 0)),
        scratch_shapes=[pltpu.VMEM((feeds // 64, width * N1 * 8, 128), jnp.float32)],
        compiler_params=pltpu.CompilerParams(vmem_limit_bytes=VMEM),
        name="finish",
    )(*mine)


def solution(mesh):
    chan, blk = mesh.shape["chan"], mesh.shape["blk"]
    return jax.shard_map(
        functools.partial(on_device, chan, blk),
        mesh=mesh,
        in_specs=(P("blk", "chan"), P()),
        out_specs=P(None, "blk", None, "chan"),
        check_vma=False,
    )
```

```python
import functools
import math

import jax
import jax.numpy as jnp
import numpy as np
from jax import lax
from jax.experimental import pallas as pl
from jax.experimental.pallas import tpu as pltpu
from jax.sharding import PartitionSpec as P

TAPS = 8
L = 4096
C = 2048
N2 = 128
N1 = L // N2
HALF = C // N1
VMEM = 56 * 1024 * 1024


def tables():
    n2 = np.arange(N2)
    angle = 2.0 * np.pi * (np.arange(N1)[:, None] * n2[None, :] % L) / L
    twiddle = np.stack([np.cos(angle), np.sin(angle)]).astype(np.float32)
    angle = 2.0 * np.pi * (np.arange(HALF)[:, None] * n2[None, :] % N2) / N2
    cos, sin = np.cos(angle) / math.sqrt(L), np.sin(angle) / math.sqrt(L)
    matrix = np.block([[cos, sin], [-sin, cos]])
    high = matrix.astype(jnp.bfloat16)
    low = (matrix - high.astype(np.float64)).astype(jnp.bfloat16)
    return twiddle, np.concatenate([low, high])


def times(scale, value):
    return None if value is None else scale * value


def plus(a, b):
    return b if a is None else a if b is None else a + b


def minus(a, b):
    return a if b is None else -b if a is None else a - b


def real_dft(values):
    n = len(values)
    if n == 1:
        return [(values[0], None)]
    half = n // 2
    even, odd = real_dft(values[0::2]), real_dft(values[1::2])
    result = [None] * (half + 1)
    for k in range(half // 2 + 1):
        (er, ei), (odr, odi) = even[k], odd[k]
        if k == 0:
            tr, ti = odr, odi
        elif 4 * k == n:
            tr, ti = odi, -odr
        else:
            c, s = math.cos(2 * math.pi * k / n), math.sin(2 * math.pi * k / n)
            tr = plus(times(c, odr), times(s, odi))
            ti = minus(times(c, odi), times(s, odr))
        result[half - k] = (minus(er, tr), minus(ti, ei))
        result[k] = (plus(er, tr), plus(ei, ti))
    return result


def fir_stage(volt, halo, taps, filtered, frames):
    first, end = frames

    @pl.loop(0, N1)
    def _(n1):
        lane = pl.multiple_of(n1 * N2, N2)
        weights = [jnp.broadcast_to(taps[t : t + 1, pl.ds(lane, N2)], (8, N2)) for t in range(TAPS)]

        def frame(f):
            if f < 0:
                return halo[:, pl.ds((f + TAPS - 1) * L + lane, N2)].astype(jnp.float32)
            return volt[:, pl.ds(f * L + lane, N2)].astype(jnp.float32)

        window = [frame(f) for f in range(first - TAPS + 1, first)]
        for f in range(end - first):
            window.append(frame(first + f))
            total = weights[0] * window[f]
            for t in range(1, TAPS):
                total = total + weights[t] * window[f + t]
            filtered[(first + f) * N1 + n1] = total


def first_stage(filtered, twiddle, turned, part, frames):
    @pl.loop(0, frames)
    def _(f):
        spectrum = real_dft([filtered[(part * frames + f) * N1 + n1] for n1 in range(N1)])
        rows = pl.ds(pl.multiple_of(f * 8, 8), 8)
        for k1 in range(N1):
            if 2 * k1 <= N1:
                zr, zi = spectrum[k1]
            else:
                zr, zi = spectrum[N1 - k1]
                zi = -zi
            c = twiddle[0, k1 : k1 + 1, :]
            s = twiddle[1, k1 : k1 + 1, :]
            if k1 == 0:
                re, im = zr, jnp.zeros_like(zr)
            elif zi is None:
                re, im = c * zr, -(s * zr)
            else:
                re, im = c * zr + s * zi, c * zi - s * zr
            turned[part * N1 + k1, rows, pl.ds(0, N2)] = re
            turned[part * N1 + k1, rows, pl.ds(N2, N2)] = im


def second_stage(turned, first, second, table):
    contract = (((1,), (1,)), ((), ()))
    z = jnp.concatenate([turned[first], turned[second]], axis=0)
    zh = z.astype(jnp.bfloat16)
    zl = (z - zh.astype(jnp.float32)).astype(jnp.bfloat16)
    both = lax.dot_general(table[...], zh, contract, preferred_element_type=jnp.float32)
    rest = lax.dot_general(table[2 * HALF :], zl, contract, preferred_element_type=jnp.float32)
    out = both[2 * HALF :] + (both[: 2 * HALF] + rest)
    return [value.astype(jnp.bfloat16) for value in swap_halves(out[:HALF], out[HALF:])]


def regroup(groups, lane):
    count = len(groups)
    d = 1
    while d < count:
        low_side = (lane & d) == 0
        result = list(groups)
        for g in range(count):
            if g & d == 0:
                a, b = groups[g], groups[g | d]
                result[g] = jnp.where(low_side, a, pltpu.roll(b, d, 1))
                result[g | d] = jnp.where(low_side, pltpu.roll(a, 128 - d, 1), b)
        groups = result
        d *= 2
    return groups


def gather_feeds(get, count, chan, width, start, grouped):
    lane = lax.broadcasted_iota(jnp.int32, (width, 128), 1)

    @pl.loop(0, count, unroll=count <= 8)
    def _(at):
        arrays = [get(c, at, part).astype(jnp.float32) for part in range(2) for c in range(chan)]
        for feed, value in enumerate(regroup(arrays, lane)):
            row = pl.multiple_of(((start + at) * 8 + feed) * width, width)
            grouped[pl.ds(row, width), :] = value


def sides(grouped, ch, feeds, width):
    lane = lax.broadcasted_iota(jnp.int32, (feeds, 128), 1)
    value = grouped[pl.ds(ch, feeds, stride=width), :]
    other = pltpu.roll(value, 64, 1)
    other = jnp.where(lane < 64, -other, other)
    return value.astype(jnp.bfloat16), other.astype(jnp.bfloat16)


def product(left, right):
    return lax.dot_general(left, right, (((1,), (1,)), ((), ())), preferred_element_type=jnp.float32)


def paired(lefts, rights, order):
    rows = []
    for part in range(2):
        for one in order:
            zero = jnp.zeros_like(rights[one][part])
            rows.append(jnp.concatenate([rights[0][part] if one == 0 else zero, rights[1][part] if one else zero], axis=1))
    return product(jnp.concatenate(lefts, axis=1), jnp.concatenate(rows, axis=0))


def quad_by_channel(grouped, nearby, quad, feeds, width):
    near_feeds = feeds // 2
    full_rows, far_rows, own_rows = [], [], []
    for pair in range(2):
        lefts, rights, own_lefts, own_rights, full = [], [], [], [], []
        for one in range(2):
            ch = quad * 4 + pair * 2 + one
            value, other = sides(grouped, ch, feeds, width)
            full.append(product(value[:near_feeds], jnp.concatenate([value, other], axis=0)))
            lefts.append(value[near_feeds:])
            rights.append((value[:near_feeds], other[:near_feeds]))
            value, other = sides(nearby, ch, near_feeds, width)
            own_lefts.append(value)
            own_rights.append((value, other))
        full_rows.append(full)
        far_rows.append(paired(lefts, rights, (1, 0)))
        own_rows.append(paired(own_lefts, own_rights, (0, 1)))
    return full_rows, far_rows, own_rows


def square(value):
    turned = value.T
    other = jnp.concatenate([-turned[64:], turned[:64]], axis=0)
    right = jnp.concatenate([turned, other], axis=1).astype(jnp.bfloat16)
    out = jnp.dot(value.astype(jnp.bfloat16), right, preferred_element_type=jnp.float32)
    return out[:, :128], out[:, 128:]


def quad_of_64(grouped, nearby, quad, width):
    lane = lax.broadcasted_iota(jnp.int32, (32, 128), 1)
    low, first, third = lane < 64, lane < 32, lane < 96

    def roll(value, shift):
        return pltpu.roll(value, shift, 1)

    full_rows, far_rows = [], []
    for pair in range(2):
        ch = quad * 4 + pair * 2
        value = jnp.concatenate([grouped[pl.ds(ch + one, 64, stride=width), :] for one in range(2)], axis=0)
        re, im = square(value)
        full_rows.append(
            [
                jnp.where(low, re[:32], roll(im[:32], 64)),
                jnp.where(low, roll(re[64:96], 64), im[64:96]),
            ]
        )
        far_rows.append(
            jnp.where(
                low,
                jnp.where(first, roll(re[96:], 64), roll(re[32:64], 32)),
                jnp.where(third, im[96:], roll(im[32:64], 96)),
            )
        )
    value = jnp.concatenate([nearby[pl.ds(quad * 4 + one, 32, stride=width), :] for one in range(4)], axis=0)
    re, im = square(value)
    own_rows = [
        jnp.where(low, jnp.where(first, re[:32], re[32:64]), roll(jnp.where(first, im[:32], im[32:64]), 64)),
        jnp.where(low, roll(jnp.where(third, re[64:96], re[96:]), 64), jnp.where(third, im[64:96], im[96:])),
    ]
    return full_rows, far_rows, own_rows


def correlate(grouped, nearby, half, width, spectra_count, near, far):
    feeds = 16 * half
    scale = 1.0 / spectra_count

    @pl.loop(0, width // 4, unroll=True)
    def _(quad):
        if feeds == 64:
            full_rows, far_rows, own_rows = quad_of_64(grouped, nearby, quad, width)
        else:
            full_rows, far_rows, own_rows = quad_by_channel(grouped, nearby, quad, feeds, width)
        for b in range(half):
            cut = slice(b * 8, b * 8 + 8)

            def put(ref, row, first, second):
                rows = jnp.concatenate([first[cut], second[cut]], axis=0) * scale
                ref[b, pl.ds(pl.multiple_of(row, 16), 16), :] = rows.astype(jnp.bfloat16)

            for pair in range(2):
                put(near, (quad * 2 + pair) * 16, *full_rows[pair])
            put(near, width * 8 + quad * 16, *own_rows)
            put(far, quad * 16, *far_rows)


def exchange_kernel(
    sizes, volt, taps, twiddle, table, out_near, out_far,
    halo, filtered, turned, to_far_late, to_far, to_near_late, to_near,
    from_far_late, from_far, from_near_late, from_near, grouped, nearby, near, far,
    halo_sems, send_sems, seen_sems, product_sems, out_sems,
):
    frames, chan, blk = sizes
    parts, half = chan * blk, blk // 2
    width = HALF // chan
    per = N1 // blk
    chunks, held = to_far.shape[0], per // to_far.shape[0]
    c, b = lax.axis_index("chan"), lax.axis_index("blk")
    side, spot = lax.div(b, half), lax.rem(b, half)
    barrier = pltpu.get_barrier_semaphore()

    def remote(src, dst, send_sem, recv_sem, to_c, to_b):
        return pltpu.make_async_remote_copy(
            src_ref=src,
            dst_ref=dst,
            send_sem=send_sem,
            recv_sem=recv_sem,
            device_id={"chan": to_c, "blk": to_b},
            device_id_type=pl.DeviceIdType.MESH,
        )

    @pl.loop(1, parts)
    def _(d):
        other = lax.rem(c * blk + b + d, parts)
        pl.semaphore_signal(
            barrier,
            inc=1,
            device_id={"chan": lax.div(other, blk), "blk": lax.rem(other, blk)},
            device_id_type=pl.DeviceIdType.MESH,
        )

    @pl.when(c == 0)
    def _():
        halo[...] = jnp.zeros_like(halo)

    def send(part, q, slot, held, to_far, to_near, from_far, from_near):
        rows = held * width

        @pl.loop(0, half)
        def _(t):
            at = lax.rem(spot + 1 + t, half)
            near_b, far_b = side * half + at, (1 - side) * half + at
            bases = [part * N1 + to_b * per + q * held for to_b in (far_b, near_b)]
            single = second_stage(turned, *bases, table) if held == 1 else None
            for one, (to_b, refs) in enumerate(((far_b, ((to_far, 0), (to_near, rows))), (near_b, ((to_near, 0),)))):
                values = [single[one]] if held == 1 else []
                for first in range(0, held - 1, 2):
                    values += second_stage(turned, bases[one] + first, bases[one] + first + 1, table)
                for kk in range(held):
                    for to_c in range(chan):
                        value = values[kk][to_c * width : (to_c + 1) * width]
                        for ref, start in refs:
                            ref[q, to_c * half + at, pl.ds(start + kk * width, width), :] = value
                if to_b is far_b:
                    for u in range(chan):
                        to_c = lax.rem(c + u, chan)
                        block = to_far.at[q, to_c * half + at]
                        dst = from_far.at[q, c * half + spot]
                        remote(block, dst, send_sems.at[0, slot], seen_sems.at[0, slot], to_c, far_b).start()
            for u in range(chan):
                to_c = lax.rem(c + u, chan)
                block, dst = to_near.at[q, to_c * half + at], from_near.at[q, c * half + spot]
                copy = remote(block, dst, send_sems.at[1, slot], seen_sems.at[1, slot], to_c, near_b)
                if u == 0:
                    pl.when(at != spot)(copy.start)
                    pl.when(at == spot)(pltpu.make_async_copy(block, dst, seen_sems.at[1, slot]).start)
                else:
                    copy.start()

    count = frames // 2
    fir_stage(volt, halo, taps, filtered, (count, frames))
    pl.semaphore_wait(barrier, parts - 1)
    last = volt.at[:, pl.ds((frames - TAPS + 1) * L, (TAPS - 1) * L)]
    halo_copy = remote(last, halo, halo_sems.at[0], halo_sems.at[1], lax.rem(c + 1, chan), b)

    @pl.when(c < chan - 1)
    def _():
        halo_copy.start()

    first_stage(filtered, twiddle, turned, 1, count)
    send(1, 0, 0, per, to_far_late, to_near_late, from_far_late, from_near_late)

    @pl.when(c > 0)
    def _():
        halo_copy.wait_recv()

    fir_stage(volt, halo, taps, filtered, (0, count))
    first_stage(filtered, twiddle, turned, 0, count)
    for q in range(chunks):
        send(0, q, 1 + q, held, to_far, to_near, from_far, from_near)

    def arrived(ref, kind, q, slot):
        pltpu.make_async_copy(ref.at[q], ref.at[q], seen_sems.at[kind, slot]).wait()

    arrived(from_far_late, 0, 0, 0)
    arrived(from_near_late, 1, 0, 0)
    for q in range(chunks):
        arrived(from_far, 0, q, 1 + q)
        arrived(from_near, 1, q, 1 + q)
        for kk in range(held):
            index = q * held + kk

            def reader(late, early, second):
                def get(from_c, at, part):
                    source = from_c * half + at
                    if part == 1:
                        return late[0, source, pl.ds((second * per + index) * width, width), :]
                    return early[q, source, pl.ds((second * held + kk) * width, width), :]

                return get

            gather_feeds(reader(from_near_late, from_near, 0), half, chan, width, 0, grouped)
            gather_feeds(reader(from_far_late, from_far, 0), half, chan, width, half, grouped)
            gather_feeds(reader(from_near_late, from_near, 1), half, chan, width, 0, nearby)
            correlate(grouped, nearby, half, width, frames * chan, near.at[index], far.at[index])

            @pl.loop(0, half)
            def _(t):
                at = lax.rem(spot + 1 + t, half)
                near_b, far_b = side * half + at, (1 - side) * half + at
                remote(
                    far.at[index, at], out_far.at[index, spot], product_sems.at[1, index], out_sems.at[1], c, far_b
                ).start()
                copy = remote(
                    near.at[index, at], out_near.at[index, spot], product_sems.at[0, index], out_sems.at[0], c, near_b
                )
                pl.when(at != spot)(copy.start)

            pltpu.make_async_copy(near.at[index, spot], out_near.at[index, spot], out_sems.at[0]).start()

    pltpu.make_async_copy(out_near, out_near, out_sems.at[0]).wait()
    pltpu.make_async_copy(out_far, out_far, out_sems.at[1]).wait()
    for slot in range(1 + chunks):
        q = max(slot - 1, 0)
        piece = (to_far if slot else to_far_late).at[q]
        pltpu.make_async_copy(piece, piece, send_sems.at[0, slot]).wait()
        piece = (to_near if slot else to_near_late).at[q, pl.ds(0, chan * half - 1)]
        pltpu.make_async_copy(piece, piece, send_sems.at[1, slot]).wait()
    for index in range(per):
        piece = near.at[index, pl.ds(0, half - 1)]
        pltpu.make_async_copy(piece, piece, product_sems.at[0, index]).wait()
        pltpu.make_async_copy(far.at[index], far.at[index], product_sems.at[1, index]).wait()

    @pl.when(c < chan - 1)
    def _():
        halo_copy.wait_send()


def swap_halves(first, second):
    low_side = lax.broadcasted_iota(jnp.int32, first.shape, 1) < 64
    return [
        jnp.where(low_side, first, pltpu.roll(second, 64, 1)),
        jnp.where(low_side, pltpu.roll(first, 64, 1), second),
    ]


def join(own, other, feeds):
    count = feeds // 2
    if count % 128 == 0:
        cuts = [slice(at, at + count) for at in range(0, 2 * feeds, count)]
        return [
            jnp.concatenate([own[:, cuts[0]], other[:, cuts[1]], own[:, cuts[2]], other[:, cuts[3]]], axis=1),
            jnp.concatenate([own[:, cuts[1]], other[:, cuts[0]], own[:, cuts[3]], other[:, cuts[2]]], axis=1),
        ]
    even = lax.broadcasted_iota(jnp.int32, own.shape, 1) // count % 2 == 0
    return [
        jnp.where(even, own, other),
        jnp.where(even, pltpu.roll(own, 2 * feeds - count, 1), pltpu.roll(other, count, 1)),
    ]


def finish_kernel(blk, per, width, feeds, near, far, out, wide, built, sems):
    half = blk // 2
    side = lax.div(lax.axis_index("blk"), half)

    def put(k2, k1, rows):
        row = pl.multiple_of((k2 * N1 + k1) * 8, 8)
        for first in range(0, 2 * feeds, 128):
            wide[first // 128, pl.ds(row, 8), :] = rows[:, first : first + 128]

    @pl.loop(0, half)
    def _(at):
        near_b, far_b = side * half + at, (1 - side) * half + at
        for kk in range(per):
            value = near[kk, at].astype(jnp.float32)
            other = far[kk, at].astype(jnp.float32)
            for k2 in range(width):
                put(k2, near_b * per + kk, value[k2 * 8 : k2 * 8 + 8])
            for pair in range(width // 2):
                own = value[(width + pair) * 8 : (width + pair) * 8 + 8]
                for one, rows in enumerate(join(own, other[pair * 8 : pair * 8 + 8], feeds)):
                    put(2 * pair + one, far_b * per + kk, rows)

    count = feeds // 2
    piece = min(count, 128)
    copies = []
    for i in range(8):
        for block in range(0, width * N1, 128):
            for first in range(0, 2 * feeds, 128):
                tile = wide[first // 128, pl.ds(block * 8 + i, 128, stride=8), :].T
                for at in range(0, 128, piece):
                    part, rest = divmod(first + at, feeds)
                    which, j = divmod(rest, count)
                    start = (side if which == 0 else 1 - side) * count + j
                    rows = pl.ds(pl.multiple_of(start, piece), piece)
                    built[i, part, rows, pl.ds(block, 128)] = tile[at : at + piece]
        for part in range(2):
            copies.append(pltpu.make_async_copy(built.at[i, part], out.at[part, i], sems.at[i, part]))
            copies[-1].start()
    for copy in copies:
        copy.wait()


def whole(count):
    return [pl.BlockSpec(memory_space=pltpu.VMEM)] * count


def on_device(chan, blk, voltages, fir_taps):
    frames = voltages.shape[1] // L
    parts, half = chan * blk, blk // 2
    feeds = blk * 8
    per, width = N1 // blk, HALF // chan
    chunks = per
    twiddle, table = tables()
    dma = pltpu.SemaphoreType.DMA
    blocks = [
        pltpu.VMEM((pieces, parts // 2, sets * width * per // pieces, 128), jnp.bfloat16)
        for sets in (1, 2)
        for pieces in (1, chunks)
    ]
    any_place = pl.BlockSpec(memory_space=pl.ANY)
    near = (per, half, width * 12, 2 * feeds)
    far = (per, half, width * 4, 2 * feeds)
    mine = pl.pallas_call(
        functools.partial(exchange_kernel, (frames, chan, blk)),
        out_shape=[jax.ShapeDtypeStruct(near, jnp.bfloat16), jax.ShapeDtypeStruct(far, jnp.bfloat16)],
        in_specs=whole(4),
        out_specs=[any_place, any_place],
        scratch_shapes=[
            pltpu.VMEM((8, (TAPS - 1) * L), jnp.bfloat16),
            pltpu.VMEM((frames * N1, 8, N2), jnp.float32),
            pltpu.VMEM((2 * N1, 4 * frames, 2 * N2), jnp.float32),
            *blocks,
            *blocks,
            pltpu.VMEM((feeds * width, 128), jnp.float32),
            pltpu.VMEM((feeds // 2 * width, 128), jnp.float32),
            pltpu.VMEM(near, jnp.bfloat16),
            pltpu.VMEM(far, jnp.bfloat16),
            dma((2,)),
            dma((2, 1 + chunks)),
            dma((2, 1 + chunks)),
            dma((2, per)),
            dma((2,)),
        ],
        compiler_params=pltpu.CompilerParams(vmem_limit_bytes=VMEM, collective_id=0, has_side_effects=True),
        name="exchange",
    )(voltages, fir_taps, jnp.asarray(twiddle), jnp.asarray(table))
    return pl.pallas_call(
        functools.partial(finish_kernel, blk, per, width, feeds),
        out_shape=jax.ShapeDtypeStruct((2, 8, feeds, width * N1), jnp.float32),
        in_specs=whole(2),
        out_specs=any_place,
        scratch_shapes=[
            pltpu.VMEM((feeds // 64, width * N1 * 8, 128), jnp.float32),
            pltpu.VMEM((8, 2, feeds, width * N1), jnp.float32),
            dma((8, 2)),
        ],
        compiler_params=pltpu.CompilerParams(vmem_limit_bytes=VMEM),
        name="finish",
    )(*mine)


def solution(mesh):
    chan, blk = mesh.shape["chan"], mesh.shape["blk"]
    return jax.shard_map(
        functools.partial(on_device, chan, blk),
        mesh=mesh,
        in_specs=(P("blk", "chan"), P()),
        out_specs=P(None, "blk", None, "chan"),
        check_vma=False,
    )
```

```python
import functools
import math

import jax
import jax.numpy as jnp
import numpy as np
from jax import lax
from jax.experimental import pallas as pl
from jax.experimental.pallas import tpu as pltpu
from jax.sharding import PartitionSpec as P

TAPS = 8
L = 4096
C = 2048
N2 = 128
N1 = L // N2
HALF = C // N1
VMEM = 56 * 1024 * 1024


def tables():
    n2 = np.arange(N2)
    angle = 2.0 * np.pi * (np.arange(N1)[:, None] * n2[None, :] % L) / L
    twiddle = np.stack([np.cos(angle), np.sin(angle)]).astype(np.float32)
    angle = 2.0 * np.pi * (np.arange(HALF)[:, None] * n2[None, :] % N2) / N2
    cos, sin = np.cos(angle) / math.sqrt(L), np.sin(angle) / math.sqrt(L)
    matrix = np.block([[cos, sin], [-sin, cos]])
    high = matrix.astype(jnp.bfloat16)
    low = (matrix - high.astype(np.float64)).astype(jnp.bfloat16)
    return twiddle, np.concatenate([low, high])


def times(scale, value):
    return None if value is None else scale * value


def plus(a, b):
    return b if a is None else a if b is None else a + b


def minus(a, b):
    return a if b is None else -b if a is None else a - b


def real_dft(values):
    n = len(values)
    if n == 1:
        return [(values[0], None)]
    half = n // 2
    even, odd = real_dft(values[0::2]), real_dft(values[1::2])
    result = [None] * (half + 1)
    for k in range(half // 2 + 1):
        (er, ei), (odr, odi) = even[k], odd[k]
        if k == 0:
            tr, ti = odr, odi
        elif 4 * k == n:
            tr, ti = odi, -odr
        else:
            c, s = math.cos(2 * math.pi * k / n), math.sin(2 * math.pi * k / n)
            tr = plus(times(c, odr), times(s, odi))
            ti = minus(times(c, odi), times(s, odr))
        result[half - k] = (minus(er, tr), minus(ti, ei))
        result[k] = (plus(er, tr), plus(ei, ti))
    return result


def fir_stage(volt, halo, taps, filtered, frames):
    first, end = frames

    @pl.loop(0, N1)
    def _(n1):
        lane = pl.multiple_of(n1 * N2, N2)
        weights = [jnp.broadcast_to(taps[t : t + 1, pl.ds(lane, N2)], (8, N2)) for t in range(TAPS)]

        def frame(f):
            if f < 0:
                return halo[:, pl.ds((f + TAPS - 1) * L + lane, N2)].astype(jnp.float32)
            return volt[:, pl.ds(f * L + lane, N2)].astype(jnp.float32)

        window = [frame(f) for f in range(first - TAPS + 1, first)]
        for f in range(end - first):
            window.append(frame(first + f))
            total = weights[0] * window[f]
            for t in range(1, TAPS):
                total = total + weights[t] * window[f + t]
            filtered[(first + f) * N1 + n1] = total


def first_stage(filtered, twiddle, turned, part, frames):
    @pl.loop(0, frames)
    def _(f):
        spectrum = real_dft([filtered[(part * frames + f) * N1 + n1] for n1 in range(N1)])
        rows = pl.ds(pl.multiple_of(f * 8, 8), 8)
        for k1 in range(N1):
            if 2 * k1 <= N1:
                zr, zi = spectrum[k1]
            else:
                zr, zi = spectrum[N1 - k1]
                zi = -zi
            c = twiddle[0, k1 : k1 + 1, :]
            s = twiddle[1, k1 : k1 + 1, :]
            if k1 == 0:
                re, im = zr, jnp.zeros_like(zr)
            elif zi is None:
                re, im = c * zr, -(s * zr)
            else:
                re, im = c * zr + s * zi, c * zi - s * zr
            turned[part * N1 + k1, rows, pl.ds(0, N2)] = re
            turned[part * N1 + k1, rows, pl.ds(N2, N2)] = im


def second_stage(turned, first, second, table):
    contract = (((1,), (1,)), ((), ()))
    z = jnp.concatenate([turned[first], turned[second]], axis=0)
    zh = z.astype(jnp.bfloat16)
    zl = (z - zh.astype(jnp.float32)).astype(jnp.bfloat16)
    both = lax.dot_general(table[...], zh, contract, preferred_element_type=jnp.float32)
    rest = lax.dot_general(table[2 * HALF :], zl, contract, preferred_element_type=jnp.float32)
    out = both[2 * HALF :] + (both[: 2 * HALF] + rest)
    return [value.astype(jnp.bfloat16) for value in swap_halves(out[:HALF], out[HALF:])]


def regroup(groups, lane):
    count = len(groups)
    d = 1
    while d < count:
        low_side = (lane & d) == 0
        result = list(groups)
        for g in range(count):
            if g & d == 0:
                a, b = groups[g], groups[g | d]
                result[g] = jnp.where(low_side, a, pltpu.roll(b, d, 1))
                result[g | d] = jnp.where(low_side, pltpu.roll(a, 128 - d, 1), b)
        groups = result
        d *= 2
    return groups


def gather_feeds(get, count, chan, width, start, grouped):
    lane = lax.broadcasted_iota(jnp.int32, (width, 128), 1)

    @pl.loop(0, count, unroll=count <= 8)
    def _(at):
        arrays = [get(c, at, part).astype(jnp.float32) for part in range(2) for c in range(chan)]
        for feed, value in enumerate(regroup(arrays, lane)):
            row = pl.multiple_of(((start + at) * 8 + feed) * width, width)
            grouped[pl.ds(row, width), :] = value


def sides(grouped, ch, feeds, width):
    lane = lax.broadcasted_iota(jnp.int32, (feeds, 128), 1)
    value = grouped[pl.ds(ch, feeds, stride=width), :]
    other = pltpu.roll(value, 64, 1)
    other = jnp.where(lane < 64, -other, other)
    return value.astype(jnp.bfloat16), other.astype(jnp.bfloat16)


def product(left, right):
    return lax.dot_general(left, right, (((1,), (1,)), ((), ())), preferred_element_type=jnp.float32)


def paired(lefts, rights, order):
    rows = []
    for part in range(2):
        for one in order:
            zero = jnp.zeros_like(rights[one][part])
            rows.append(jnp.concatenate([rights[0][part] if one == 0 else zero, rights[1][part] if one else zero], axis=1))
    return product(jnp.concatenate(lefts, axis=1), jnp.concatenate(rows, axis=0))


def quad_by_channel(grouped, nearby, quad, feeds, width):
    near_feeds = feeds // 2
    full_rows, far_rows, own_rows = [], [], []
    for pair in range(2):
        lefts, rights, own_lefts, own_rights, full = [], [], [], [], []
        for one in range(2):
            ch = quad * 4 + pair * 2 + one
            value, other = sides(grouped, ch, feeds, width)
            full.append(product(value[:near_feeds], jnp.concatenate([value, other], axis=0)))
            lefts.append(value[near_feeds:])
            rights.append((value[:near_feeds], other[:near_feeds]))
            value, other = sides(nearby, ch, near_feeds, width)
            own_lefts.append(value)
            own_rights.append((value, other))
        full_rows.append(full)
        far_rows.append(paired(lefts, rights, (1, 0)))
        own_rows.append(paired(own_lefts, own_rights, (0, 1)))
    return full_rows, far_rows, own_rows


def square(value):
    turned = value.T
    other = jnp.concatenate([-turned[64:], turned[:64]], axis=0)
    right = jnp.concatenate([turned, other], axis=1).astype(jnp.bfloat16)
    out = jnp.dot(value.astype(jnp.bfloat16), right, preferred_element_type=jnp.float32)
    return out[:, :128], out[:, 128:]


def quad_of_64(grouped, nearby, quad, width):
    lane = lax.broadcasted_iota(jnp.int32, (32, 128), 1)
    low, first, third = lane < 64, lane < 32, lane < 96

    def roll(value, shift):
        return pltpu.roll(value, shift, 1)

    full_rows, far_rows = [], []
    for pair in range(2):
        ch = quad * 4 + pair * 2
        value = jnp.concatenate([grouped[pl.ds(ch + one, 64, stride=width), :] for one in range(2)], axis=0)
        re, im = square(value)
        full_rows.append(
            [
                jnp.where(low, re[:32], roll(im[:32], 64)),
                jnp.where(low, roll(re[64:96], 64), im[64:96]),
            ]
        )
        far_rows.append(
            jnp.where(
                low,
                jnp.where(first, roll(re[96:], 64), roll(re[32:64], 32)),
                jnp.where(third, im[96:], roll(im[32:64], 96)),
            )
        )
    value = jnp.concatenate([nearby[pl.ds(quad * 4 + one, 32, stride=width), :] for one in range(4)], axis=0)
    re, im = square(value)
    own_rows = [
        jnp.where(low, jnp.where(first, re[:32], re[32:64]), roll(jnp.where(first, im[:32], im[32:64]), 64)),
        jnp.where(low, roll(jnp.where(third, re[64:96], re[96:]), 64), jnp.where(third, im[64:96], im[96:])),
    ]
    return full_rows, far_rows, own_rows


def correlate(grouped, nearby, half, width, spectra_count, near, far):
    feeds = 16 * half
    scale = 1.0 / spectra_count

    @pl.loop(0, width // 4, unroll=True)
    def _(quad):
        if feeds == 64:
            full_rows, far_rows, own_rows = quad_of_64(grouped, nearby, quad, width)
        else:
            full_rows, far_rows, own_rows = quad_by_channel(grouped, nearby, quad, feeds, width)
        for b in range(half):
            cut = slice(b * 8, b * 8 + 8)

            def put(ref, row, first, second):
                rows = jnp.concatenate([first[cut], second[cut]], axis=0) * scale
                ref[b, pl.ds(pl.multiple_of(row, 16), 16), :] = rows.astype(jnp.bfloat16)

            for pair in range(2):
                put(near, (quad * 2 + pair) * 16, *full_rows[pair])
            put(near, width * 8 + quad * 16, *own_rows)
            put(far, quad * 16, *far_rows)


def exchange_kernel(
    sizes, volt, taps, twiddle, table, out_near, out_far,
    halo, filtered, turned, to_far_late, to_far, to_near_late, to_near,
    from_far_late, from_far, from_near_late, from_near, grouped, nearby, near, far,
    halo_sems, send_sems, seen_sems, product_sems, out_sems,
):
    frames, chan, blk = sizes
    parts, half = chan * blk, blk // 2
    width = HALF // chan
    per = N1 // blk
    chunks, held = to_far.shape[0], per // to_far.shape[0]
    c, b = lax.axis_index("chan"), lax.axis_index("blk")
    side, spot = lax.div(b, half), lax.rem(b, half)
    barrier = pltpu.get_barrier_semaphore()

    def remote(src, dst, send_sem, recv_sem, to_c, to_b):
        return pltpu.make_async_remote_copy(
            src_ref=src,
            dst_ref=dst,
            send_sem=send_sem,
            recv_sem=recv_sem,
            device_id={"chan": to_c, "blk": to_b},
            device_id_type=pl.DeviceIdType.MESH,
        )

    @pl.loop(1, parts)
    def _(d):
        other = lax.rem(c * blk + b + d, parts)
        pl.semaphore_signal(
            barrier,
            inc=1,
            device_id={"chan": lax.div(other, blk), "blk": lax.rem(other, blk)},
            device_id_type=pl.DeviceIdType.MESH,
        )

    @pl.when(c == 0)
    def _():
        halo[...] = jnp.zeros_like(halo)

    def send(part, q, slot, held, to_far, to_near, from_far, from_near):
        rows = held * width

        @pl.loop(0, half)
        def _(t):
            at = lax.rem(spot + 1 + t, half)
            near_b, far_b = side * half + at, (1 - side) * half + at
            bases = [part * N1 + to_b * per + q * held for to_b in (far_b, near_b)]
            single = second_stage(turned, *bases, table) if held == 1 else None
            for one, (to_b, refs) in enumerate(((far_b, ((to_far, 0), (to_near, rows))), (near_b, ((to_near, 0),)))):
                values = [single[one]] if held == 1 else []
                for first in range(0, held - 1, 2):
                    values += second_stage(turned, bases[one] + first, bases[one] + first + 1, table)
                for kk in range(held):
                    for to_c in range(chan):
                        value = values[kk][to_c * width : (to_c + 1) * width]
                        for ref, start in refs:
                            ref[q, to_c * half + at, pl.ds(start + kk * width, width), :] = value
                if to_b is far_b:
                    for u in range(chan):
                        to_c = lax.rem(c + u, chan)
                        block = to_far.at[q, to_c * half + at]
                        dst = from_far.at[q, c * half + spot]
                        remote(block, dst, send_sems.at[0, slot], seen_sems.at[0, slot], to_c, far_b).start()
            for u in range(chan):
                to_c = lax.rem(c + u, chan)
                block, dst = to_near.at[q, to_c * half + at], from_near.at[q, c * half + spot]
                copy = remote(block, dst, send_sems.at[1, slot], seen_sems.at[1, slot], to_c, near_b)
                if u == 0:
                    pl.when(at != spot)(copy.start)
                    pl.when(at == spot)(pltpu.make_async_copy(block, dst, seen_sems.at[1, slot]).start)
                else:
                    copy.start()

    count = frames // 2
    fir_stage(volt, halo, taps, filtered, (count, frames))
    pl.semaphore_wait(barrier, parts - 1)
    last = volt.at[:, pl.ds((frames - TAPS + 1) * L, (TAPS - 1) * L)]
    halo_copy = remote(last, halo, halo_sems.at[0], halo_sems.at[1], lax.rem(c + 1, chan), b)

    @pl.when(c < chan - 1)
    def _():
        halo_copy.start()

    first_stage(filtered, twiddle, turned, 1, count)
    send(1, 0, 0, per, to_far_late, to_near_late, from_far_late, from_near_late)

    @pl.when(c > 0)
    def _():
        halo_copy.wait_recv()

    fir_stage(volt, halo, taps, filtered, (0, count))
    first_stage(filtered, twiddle, turned, 0, count)
    for q in range(chunks):
        send(0, q, 1 + q, held, to_far, to_near, from_far, from_near)

    def arrived(ref, kind, q, slot):
        pltpu.make_async_copy(ref.at[q], ref.at[q], seen_sems.at[kind, slot]).wait()

    arrived(from_far_late, 0, 0, 0)
    arrived(from_near_late, 1, 0, 0)
    for q in range(chunks):
        arrived(from_far, 0, q, 1 + q)
        arrived(from_near, 1, q, 1 + q)
        for kk in range(held):
            index = q * held + kk

            def reader(late, early, second):
                def get(from_c, at, part):
                    source = from_c * half + at
                    if part == 1:
                        return late[0, source, pl.ds((second * per + index) * width, width), :]
                    return early[q, source, pl.ds((second * held + kk) * width, width), :]

                return get

            gather_feeds(reader(from_near_late, from_near, 0), half, chan, width, 0, grouped)
            gather_feeds(reader(from_far_late, from_far, 0), half, chan, width, half, grouped)
            gather_feeds(reader(from_near_late, from_near, 1), half, chan, width, 0, nearby)
            correlate(grouped, nearby, half, width, frames * chan, near.at[index], far.at[index])

            @pl.loop(0, half)
            def _(t):
                at = lax.rem(spot + 1 + t, half)
                near_b, far_b = side * half + at, (1 - side) * half + at
                remote(
                    far.at[index, at], out_far.at[index, spot], product_sems.at[1, index], out_sems.at[1], c, far_b
                ).start()
                copy = remote(
                    near.at[index, at], out_near.at[index, spot], product_sems.at[0, index], out_sems.at[0], c, near_b
                )
                pl.when(at != spot)(copy.start)

            pltpu.make_async_copy(near.at[index, spot], out_near.at[index, spot], out_sems.at[0]).start()

    pltpu.make_async_copy(out_near, out_near, out_sems.at[0]).wait()
    pltpu.make_async_copy(out_far, out_far, out_sems.at[1]).wait()
    for slot in range(1 + chunks):
        q = max(slot - 1, 0)
        piece = (to_far if slot else to_far_late).at[q]
        pltpu.make_async_copy(piece, piece, send_sems.at[0, slot]).wait()
        piece = (to_near if slot else to_near_late).at[q, pl.ds(0, chan * half - 1)]
        pltpu.make_async_copy(piece, piece, send_sems.at[1, slot]).wait()
    for index in range(per):
        piece = near.at[index, pl.ds(0, half - 1)]
        pltpu.make_async_copy(piece, piece, product_sems.at[0, index]).wait()
        pltpu.make_async_copy(far.at[index], far.at[index], product_sems.at[1, index]).wait()

    @pl.when(c < chan - 1)
    def _():
        halo_copy.wait_send()


def swap_halves(first, second):
    low_side = lax.broadcasted_iota(jnp.int32, first.shape, 1) < 64
    return [
        jnp.where(low_side, first, pltpu.roll(second, 64, 1)),
        jnp.where(low_side, pltpu.roll(first, 64, 1), second),
    ]


def join(own, other, feeds):
    count = feeds // 2
    if count % 128 == 0:
        cuts = [slice(at, at + count) for at in range(0, 2 * feeds, count)]
        return [
            jnp.concatenate([own[:, cuts[0]], other[:, cuts[1]], own[:, cuts[2]], other[:, cuts[3]]], axis=1),
            jnp.concatenate([own[:, cuts[1]], other[:, cuts[0]], own[:, cuts[3]], other[:, cuts[2]]], axis=1),
        ]
    even = lax.broadcasted_iota(jnp.int32, own.shape, 1) // count % 2 == 0
    return [
        jnp.where(even, own, other),
        jnp.where(even, pltpu.roll(own, 2 * feeds - count, 1), pltpu.roll(other, count, 1)),
    ]


def finish_kernel(blk, per, width, feeds, near, far, out, wide, built, sems):
    half = blk // 2
    side = lax.div(lax.axis_index("blk"), half)

    def put(k2, k1, rows):
        row = pl.multiple_of((k2 * N1 + k1) * 8, 8)
        for first in range(0, 2 * feeds, 128):
            wide[first // 128, pl.ds(row, 8), :] = rows[:, first : first + 128]

    @pl.loop(0, half)
    def _(at):
        near_b, far_b = side * half + at, (1 - side) * half + at
        for kk in range(per):
            value = near[kk, at].astype(jnp.float32)
            other = far[kk, at].astype(jnp.float32)
            for k2 in range(width):
                put(k2, near_b * per + kk, value[k2 * 8 : k2 * 8 + 8])
            for pair in range(width // 2):
                own = value[(width + pair) * 8 : (width + pair) * 8 + 8]
                for one, rows in enumerate(join(own, other[pair * 8 : pair * 8 + 8], feeds)):
                    put(2 * pair + one, far_b * per + kk, rows)

    count = feeds // 2
    piece = min(count, 128)
    copies = []
    for i in range(8):
        for block in range(0, width * N1, 128):
            for first in range(0, 2 * feeds, 128):
                tile = wide[first // 128, pl.ds(block * 8 + i, 128, stride=8), :].T
                for at in range(0, 128, piece):
                    part, rest = divmod(first + at, feeds)
                    which, j = divmod(rest, count)
                    start = (side if which == 0 else 1 - side) * count + j
                    rows = pl.ds(pl.multiple_of(start, piece), piece)
                    built[i, part, rows, pl.ds(block, 128)] = tile[at : at + piece]
        for part in range(2):
            copies.append(pltpu.make_async_copy(built.at[i, part], out.at[part, i], sems.at[i, part]))
            copies[-1].start()
    for copy in copies:
        copy.wait()


def whole(count):
    return [pl.BlockSpec(memory_space=pltpu.VMEM)] * count


def on_device(chan, blk, voltages, fir_taps):
    frames = voltages.shape[1] // L
    parts, half = chan * blk, blk // 2
    feeds = blk * 8
    per, width = N1 // blk, HALF // chan
    chunks = min(per, 2)
    twiddle, table = tables()
    dma = pltpu.SemaphoreType.DMA
    blocks = [
        pltpu.VMEM((pieces, parts // 2, sets * width * per // pieces, 128), jnp.bfloat16)
        for sets in (1, 2)
        for pieces in (1, chunks)
    ]
    any_place = pl.BlockSpec(memory_space=pl.ANY)
    near = (per, half, width * 12, 2 * feeds)
    far = (per, half, width * 4, 2 * feeds)
    mine = pl.pallas_call(
        functools.partial(exchange_kernel, (frames, chan, blk)),
        out_shape=[jax.ShapeDtypeStruct(near, jnp.bfloat16), jax.ShapeDtypeStruct(far, jnp.bfloat16)],
        in_specs=whole(4),
        out_specs=[any_place, any_place],
        scratch_shapes=[
            pltpu.VMEM((8, (TAPS - 1) * L), jnp.bfloat16),
            pltpu.VMEM((frames * N1, 8, N2), jnp.float32),
            pltpu.VMEM((2 * N1, 4 * frames, 2 * N2), jnp.float32),
            *blocks,
            *blocks,
            pltpu.VMEM((feeds * width, 128), jnp.float32),
            pltpu.VMEM((feeds // 2 * width, 128), jnp.float32),
            pltpu.VMEM(near, jnp.bfloat16),
            pltpu.VMEM(far, jnp.bfloat16),
            dma((2,)),
            dma((2, 1 + chunks)),
            dma((2, 1 + chunks)),
            dma((2, per)),
            dma((2,)),
        ],
        compiler_params=pltpu.CompilerParams(vmem_limit_bytes=VMEM, collective_id=0, has_side_effects=True),
        name="exchange",
    )(voltages, fir_taps, jnp.asarray(twiddle), jnp.asarray(table))
    return pl.pallas_call(
        functools.partial(finish_kernel, blk, per, width, feeds),
        out_shape=jax.ShapeDtypeStruct((2, 8, feeds, width * N1), jnp.float32),
        in_specs=whole(2),
        out_specs=any_place,
        scratch_shapes=[
            pltpu.VMEM((feeds // 64, width * N1 * 8, 128), jnp.float32),
            pltpu.VMEM((8, 2, feeds, width * N1), jnp.float32),
            dma((8, 2)),
        ],
        compiler_params=pltpu.CompilerParams(vmem_limit_bytes=VMEM),
        name="finish",
    )(*mine)


def solution(mesh):
    chan, blk = mesh.shape["chan"], mesh.shape["blk"]
    return jax.shard_map(
        functools.partial(on_device, chan, blk),
        mesh=mesh,
        in_specs=(P("blk", "chan"), P()),
        out_specs=P(None, "blk", None, "chan"),
        check_vma=False,
    )
```

```python
import functools
import math

import jax
import jax.numpy as jnp
import numpy as np
from jax import lax
from jax.experimental import pallas as pl
from jax.experimental.pallas import tpu as pltpu
from jax.sharding import PartitionSpec as P

TAPS = 8
L = 4096
C = 2048
N2 = 128
N1 = L // N2
HALF = C // N1
VMEM = 56 * 1024 * 1024


def tables():
    n2 = np.arange(N2)
    angle = 2.0 * np.pi * (np.arange(N1)[:, None] * n2[None, :] % L) / L
    twiddle = np.stack([np.cos(angle), np.sin(angle)]).astype(np.float32)
    angle = 2.0 * np.pi * (np.arange(HALF)[:, None] * n2[None, :] % N2) / N2
    cos, sin = np.cos(angle) / math.sqrt(L), np.sin(angle) / math.sqrt(L)
    matrix = np.block([[cos, sin], [-sin, cos]])
    high = matrix.astype(jnp.bfloat16)
    low = (matrix - high.astype(np.float64)).astype(jnp.bfloat16)
    return twiddle, np.concatenate([low, high])


def times(scale, value):
    return None if value is None else scale * value


def plus(a, b):
    return b if a is None else a if b is None else a + b


def minus(a, b):
    return a if b is None else -b if a is None else a - b


def real_dft(values):
    n = len(values)
    if n == 1:
        return [(values[0], None)]
    half = n // 2
    even, odd = real_dft(values[0::2]), real_dft(values[1::2])
    result = [None] * (half + 1)
    for k in range(half // 2 + 1):
        (er, ei), (odr, odi) = even[k], odd[k]
        if k == 0:
            tr, ti = odr, odi
        elif 4 * k == n:
            tr, ti = odi, -odr
        else:
            c, s = math.cos(2 * math.pi * k / n), math.sin(2 * math.pi * k / n)
            tr = plus(times(c, odr), times(s, odi))
            ti = minus(times(c, odi), times(s, odr))
        result[half - k] = (minus(er, tr), minus(ti, ei))
        result[k] = (plus(er, tr), plus(ei, ti))
    return result


def fir_stage(volt, halo, taps, filtered, frames):
    first, end = frames

    @pl.loop(0, N1, unroll=2)
    def _(n1):
        lane = pl.multiple_of(n1 * N2, N2)
        weights = [jnp.broadcast_to(taps[t : t + 1, pl.ds(lane, N2)], (8, N2)) for t in range(TAPS)]

        def frame(f):
            if f < 0:
                return halo[:, pl.ds((f + TAPS - 1) * L + lane, N2)].astype(jnp.float32)
            return volt[:, pl.ds(f * L + lane, N2)].astype(jnp.float32)

        window = [frame(f) for f in range(first - TAPS + 1, first)]
        for f in range(end - first):
            window.append(frame(first + f))
            total = weights[0] * window[f]
            for t in range(1, TAPS):
                total = total + weights[t] * window[f + t]
            filtered[(first + f) * N1 + n1] = total


def first_stage(filtered, twiddle, turned, part, frames):
    @pl.loop(0, frames)
    def _(f):
        spectrum = real_dft([filtered[(part * frames + f) * N1 + n1] for n1 in range(N1)])
        rows = pl.ds(pl.multiple_of(f * 8, 8), 8)
        for k1 in range(N1):
            if 2 * k1 <= N1:
                zr, zi = spectrum[k1]
            else:
                zr, zi = spectrum[N1 - k1]
                zi = -zi
            c = twiddle[0, k1 : k1 + 1, :]
            s = twiddle[1, k1 : k1 + 1, :]
            if k1 == 0:
                re, im = zr, jnp.zeros_like(zr)
            elif zi is None:
                re, im = c * zr, -(s * zr)
            else:
                re, im = c * zr + s * zi, c * zi - s * zr
            turned[part * N1 + k1, rows, pl.ds(0, N2)] = re
            turned[part * N1 + k1, rows, pl.ds(N2, N2)] = im


def second_stage(turned, first, second, table):
    contract = (((1,), (1,)), ((), ()))
    z = jnp.concatenate([turned[first], turned[second]], axis=0)
    zh = z.astype(jnp.bfloat16)
    zl = (z - zh.astype(jnp.float32)).astype(jnp.bfloat16)
    both = lax.dot_general(table[...], zh, contract, preferred_element_type=jnp.float32)
    rest = lax.dot_general(table[2 * HALF :], zl, contract, preferred_element_type=jnp.float32)
    out = both[2 * HALF :] + (both[: 2 * HALF] + rest)
    return [value.astype(jnp.bfloat16) for value in swap_halves(out[:HALF], out[HALF:])]


def regroup(groups, lane):
    count = len(groups)
    d = 1
    while d < count:
        low_side = (lane & d) == 0
        result = list(groups)
        for g in range(count):
            if g & d == 0:
                a, b = groups[g], groups[g | d]
                result[g] = jnp.where(low_side, a, pltpu.roll(b, d, 1))
                result[g | d] = jnp.where(low_side, pltpu.roll(a, 128 - d, 1), b)
        groups = result
        d *= 2
    return groups


def gather_feeds(get, count, chan, width, start, grouped):
    lane = lax.broadcasted_iota(jnp.int32, (width, 128), 1)

    @pl.loop(0, count, unroll=count <= 8)
    def _(at):
        arrays = [get(c, at, part).astype(jnp.float32) for part in range(2) for c in range(chan)]
        for feed, value in enumerate(regroup(arrays, lane)):
            row = pl.multiple_of(((start + at) * 8 + feed) * width, width)
            grouped[pl.ds(row, width), :] = value


def sides(grouped, ch, feeds, width):
    lane = lax.broadcasted_iota(jnp.int32, (feeds, 128), 1)
    value = grouped[pl.ds(ch, feeds, stride=width), :]
    other = pltpu.roll(value, 64, 1)
    other = jnp.where(lane < 64, -other, other)
    return value.astype(jnp.bfloat16), other.astype(jnp.bfloat16)


def product(left, right):
    return lax.dot_general(left, right, (((1,), (1,)), ((), ())), preferred_element_type=jnp.float32)


def paired(lefts, rights, order):
    rows = []
    for part in range(2):
        for one in order:
            zero = jnp.zeros_like(rights[one][part])
            rows.append(jnp.concatenate([rights[0][part] if one == 0 else zero, rights[1][part] if one else zero], axis=1))
    return product(jnp.concatenate(lefts, axis=1), jnp.concatenate(rows, axis=0))


def quad_by_channel(grouped, nearby, quad, feeds, width):
    near_feeds = feeds // 2
    full_rows, far_rows, own_rows = [], [], []
    for pair in range(2):
        lefts, rights, own_lefts, own_rights, full = [], [], [], [], []
        for one in range(2):
            ch = quad * 4 + pair * 2 + one
            value, other = sides(grouped, ch, feeds, width)
            full.append(product(value[:near_feeds], jnp.concatenate([value, other], axis=0)))
            lefts.append(value[near_feeds:])
            rights.append((value[:near_feeds], other[:near_feeds]))
            value, other = sides(nearby, ch, near_feeds, width)
            own_lefts.append(value)
            own_rights.append((value, other))
        full_rows.append(full)
        far_rows.append(paired(lefts, rights, (1, 0)))
        own_rows.append(paired(own_lefts, own_rights, (0, 1)))
    return full_rows, far_rows, own_rows


def square(value):
    turned = value.T
    other = jnp.concatenate([-turned[64:], turned[:64]], axis=0)
    right = jnp.concatenate([turned, other], axis=1).astype(jnp.bfloat16)
    out = jnp.dot(value.astype(jnp.bfloat16), right, preferred_element_type=jnp.float32)
    return out[:, :128], out[:, 128:]


def quad_of_64(grouped, nearby, quad, width):
    lane = lax.broadcasted_iota(jnp.int32, (32, 128), 1)
    low, first, third = lane < 64, lane < 32, lane < 96

    def roll(value, shift):
        return pltpu.roll(value, shift, 1)

    full_rows, far_rows = [], []
    for pair in range(2):
        ch = quad * 4 + pair * 2
        value = jnp.concatenate([grouped[pl.ds(ch + one, 64, stride=width), :] for one in range(2)], axis=0)
        re, im = square(value)
        full_rows.append(
            [
                jnp.where(low, re[:32], roll(im[:32], 64)),
                jnp.where(low, roll(re[64:96], 64), im[64:96]),
            ]
        )
        far_rows.append(
            jnp.where(
                low,
                jnp.where(first, roll(re[96:], 64), roll(re[32:64], 32)),
                jnp.where(third, im[96:], roll(im[32:64], 96)),
            )
        )
    value = jnp.concatenate([nearby[pl.ds(quad * 4 + one, 32, stride=width), :] for one in range(4)], axis=0)
    re, im = square(value)
    own_rows = [
        jnp.where(low, jnp.where(first, re[:32], re[32:64]), roll(jnp.where(first, im[:32], im[32:64]), 64)),
        jnp.where(low, roll(jnp.where(third, re[64:96], re[96:]), 64), jnp.where(third, im[64:96], im[96:])),
    ]
    return full_rows, far_rows, own_rows


def correlate(grouped, nearby, half, width, spectra_count, near, far):
    feeds = 16 * half
    scale = 1.0 / spectra_count

    @pl.loop(0, width // 4, unroll=True)
    def _(quad):
        if feeds == 64:
            full_rows, far_rows, own_rows = quad_of_64(grouped, nearby, quad, width)
        else:
            full_rows, far_rows, own_rows = quad_by_channel(grouped, nearby, quad, feeds, width)
        for b in range(half):
            cut = slice(b * 8, b * 8 + 8)

            def put(ref, row, first, second):
                rows = jnp.concatenate([first[cut], second[cut]], axis=0) * scale
                ref[b, pl.ds(pl.multiple_of(row, 16), 16), :] = rows.astype(jnp.bfloat16)

            for pair in range(2):
                put(near, (quad * 2 + pair) * 16, *full_rows[pair])
            put(near, width * 8 + quad * 16, *own_rows)
            put(far, quad * 16, *far_rows)


def exchange_kernel(
    sizes, volt, taps, twiddle, table, out_near, out_far,
    halo, filtered, turned, to_far_late, to_far, to_near_late, to_near,
    from_far_late, from_far, from_near_late, from_near, grouped, nearby, near, far,
    halo_sems, send_sems, seen_sems, product_sems, out_sems,
):
    frames, chan, blk = sizes
    parts, half = chan * blk, blk // 2
    width = HALF // chan
    per = N1 // blk
    chunks, held = to_far.shape[0], per // to_far.shape[0]
    c, b = lax.axis_index("chan"), lax.axis_index("blk")
    side, spot = lax.div(b, half), lax.rem(b, half)
    barrier = pltpu.get_barrier_semaphore()

    def remote(src, dst, send_sem, recv_sem, to_c, to_b):
        return pltpu.make_async_remote_copy(
            src_ref=src,
            dst_ref=dst,
            send_sem=send_sem,
            recv_sem=recv_sem,
            device_id={"chan": to_c, "blk": to_b},
            device_id_type=pl.DeviceIdType.MESH,
        )

    @pl.loop(1, parts)
    def _(d):
        other = lax.rem(c * blk + b + d, parts)
        pl.semaphore_signal(
            barrier,
            inc=1,
            device_id={"chan": lax.div(other, blk), "blk": lax.rem(other, blk)},
            device_id_type=pl.DeviceIdType.MESH,
        )

    @pl.when(c == 0)
    def _():
        halo[...] = jnp.zeros_like(halo)

    def send(part, q, slot, held, to_far, to_near, from_far, from_near):
        rows = held * width

        @pl.loop(0, half)
        def _(t):
            at = lax.rem(spot + 1 + t, half)
            near_b, far_b = side * half + at, (1 - side) * half + at
            bases = [part * N1 + to_b * per + q * held for to_b in (far_b, near_b)]
            single = second_stage(turned, *bases, table) if held == 1 else None
            for one, (to_b, refs) in enumerate(((far_b, ((to_far, 0), (to_near, rows))), (near_b, ((to_near, 0),)))):
                values = [single[one]] if held == 1 else []
                for first in range(0, held - 1, 2):
                    values += second_stage(turned, bases[one] + first, bases[one] + first + 1, table)
                for kk in range(held):
                    for to_c in range(chan):
                        value = values[kk][to_c * width : (to_c + 1) * width]
                        for ref, start in refs:
                            ref[q, to_c * half + at, pl.ds(start + kk * width, width), :] = value
                if to_b is far_b:
                    for u in range(chan):
                        to_c = lax.rem(c + u, chan)
                        block = to_far.at[q, to_c * half + at]
                        dst = from_far.at[q, c * half + spot]
                        remote(block, dst, send_sems.at[0, slot], seen_sems.at[0, slot], to_c, far_b).start()
            for u in range(chan):
                to_c = lax.rem(c + u, chan)
                block, dst = to_near.at[q, to_c * half + at], from_near.at[q, c * half + spot]
                copy = remote(block, dst, send_sems.at[1, slot], seen_sems.at[1, slot], to_c, near_b)
                if u == 0:
                    pl.when(at != spot)(copy.start)
                    pl.when(at == spot)(pltpu.make_async_copy(block, dst, seen_sems.at[1, slot]).start)
                else:
                    copy.start()

    count = frames // 2
    fir_stage(volt, halo, taps, filtered, (count, frames))
    pl.semaphore_wait(barrier, parts - 1)
    last = volt.at[:, pl.ds((frames - TAPS + 1) * L, (TAPS - 1) * L)]
    halo_copy = remote(last, halo, halo_sems.at[0], halo_sems.at[1], lax.rem(c + 1, chan), b)

    @pl.when(c < chan - 1)
    def _():
        halo_copy.start()

    first_stage(filtered, twiddle, turned, 1, count)
    send(1, 0, 0, per, to_far_late, to_near_late, from_far_late, from_near_late)

    @pl.when(c > 0)
    def _():
        halo_copy.wait_recv()

    fir_stage(volt, halo, taps, filtered, (0, count))
    first_stage(filtered, twiddle, turned, 0, count)
    for q in range(chunks):
        send(0, q, 1 + q, held, to_far, to_near, from_far, from_near)

    def arrived(ref, kind, q, slot):
        pltpu.make_async_copy(ref.at[q], ref.at[q], seen_sems.at[kind, slot]).wait()

    arrived(from_far_late, 0, 0, 0)
    arrived(from_near_late, 1, 0, 0)
    for q in range(chunks):
        arrived(from_far, 0, q, 1 + q)
        arrived(from_near, 1, q, 1 + q)
        for kk in range(held):
            index = q * held + kk

            def reader(late, early, second):
                def get(from_c, at, part):
                    source = from_c * half + at
                    if part == 1:
                        return late[0, source, pl.ds((second * per + index) * width, width), :]
                    return early[q, source, pl.ds((second * held + kk) * width, width), :]

                return get

            gather_feeds(reader(from_near_late, from_near, 0), half, chan, width, 0, grouped)
            gather_feeds(reader(from_far_late, from_far, 0), half, chan, width, half, grouped)
            gather_feeds(reader(from_near_late, from_near, 1), half, chan, width, 0, nearby)
            correlate(grouped, nearby, half, width, frames * chan, near.at[index], far.at[index])

            @pl.loop(0, half)
            def _(t):
                at = lax.rem(spot + 1 + t, half)
                near_b, far_b = side * half + at, (1 - side) * half + at
                remote(
                    far.at[index, at], out_far.at[index, spot], product_sems.at[1, index], out_sems.at[1], c, far_b
                ).start()
                copy = remote(
                    near.at[index, at], out_near.at[index, spot], product_sems.at[0, index], out_sems.at[0], c, near_b
                )
                pl.when(at != spot)(copy.start)

            pltpu.make_async_copy(near.at[index, spot], out_near.at[index, spot], out_sems.at[0]).start()

    pltpu.make_async_copy(out_near, out_near, out_sems.at[0]).wait()
    pltpu.make_async_copy(out_far, out_far, out_sems.at[1]).wait()
    for slot in range(1 + chunks):
        q = max(slot - 1, 0)
        piece = (to_far if slot else to_far_late).at[q]
        pltpu.make_async_copy(piece, piece, send_sems.at[0, slot]).wait()
        piece = (to_near if slot else to_near_late).at[q, pl.ds(0, chan * half - 1)]
        pltpu.make_async_copy(piece, piece, send_sems.at[1, slot]).wait()
    for index in range(per):
        piece = near.at[index, pl.ds(0, half - 1)]
        pltpu.make_async_copy(piece, piece, product_sems.at[0, index]).wait()
        pltpu.make_async_copy(far.at[index], far.at[index], product_sems.at[1, index]).wait()

    @pl.when(c < chan - 1)
    def _():
        halo_copy.wait_send()


def swap_halves(first, second):
    low_side = lax.broadcasted_iota(jnp.int32, first.shape, 1) < 64
    return [
        jnp.where(low_side, first, pltpu.roll(second, 64, 1)),
        jnp.where(low_side, pltpu.roll(first, 64, 1), second),
    ]


def join(own, other, feeds):
    count = feeds // 2
    if count % 128 == 0:
        cuts = [slice(at, at + count) for at in range(0, 2 * feeds, count)]
        return [
            jnp.concatenate([own[:, cuts[0]], other[:, cuts[1]], own[:, cuts[2]], other[:, cuts[3]]], axis=1),
            jnp.concatenate([own[:, cuts[1]], other[:, cuts[0]], own[:, cuts[3]], other[:, cuts[2]]], axis=1),
        ]
    even = lax.broadcasted_iota(jnp.int32, own.shape, 1) // count % 2 == 0
    return [
        jnp.where(even, own, other),
        jnp.where(even, pltpu.roll(own, 2 * feeds - count, 1), pltpu.roll(other, count, 1)),
    ]


def finish_kernel(blk, per, width, feeds, near, far, out, wide, built, sems):
    half = blk // 2
    side = lax.div(lax.axis_index("blk"), half)

    def put(k2, k1, rows):
        row = pl.multiple_of((k2 * N1 + k1) * 8, 8)
        for first in range(0, 2 * feeds, 128):
            wide[first // 128, pl.ds(row, 8), :] = rows[:, first : first + 128]

    @pl.loop(0, half)
    def _(at):
        near_b, far_b = side * half + at, (1 - side) * half + at
        for kk in range(per):
            value = near[kk, at].astype(jnp.float32)
            other = far[kk, at].astype(jnp.float32)
            for k2 in range(width):
                put(k2, near_b * per + kk, value[k2 * 8 : k2 * 8 + 8])
            for pair in range(width // 2):
                own = value[(width + pair) * 8 : (width + pair) * 8 + 8]
                for one, rows in enumerate(join(own, other[pair * 8 : pair * 8 + 8], feeds)):
                    put(2 * pair + one, far_b * per + kk, rows)

    count = feeds // 2
    piece = min(count, 128)
    copies = []
    for i in range(8):
        for block in range(0, width * N1, 128):
            for first in range(0, 2 * feeds, 128):
                tile = wide[first // 128, pl.ds(block * 8 + i, 128, stride=8), :].T
                for at in range(0, 128, piece):
                    part, rest = divmod(first + at, feeds)
                    which, j = divmod(rest, count)
                    start = (side if which == 0 else 1 - side) * count + j
                    rows = pl.ds(pl.multiple_of(start, piece), piece)
                    built[i, part, rows, pl.ds(block, 128)] = tile[at : at + piece]
        for part in range(2):
            copies.append(pltpu.make_async_copy(built.at[i, part], out.at[part, i], sems.at[i, part]))
            copies[-1].start()
    for copy in copies:
        copy.wait()


def whole(count):
    return [pl.BlockSpec(memory_space=pltpu.VMEM)] * count


def on_device(chan, blk, voltages, fir_taps):
    frames = voltages.shape[1] // L
    parts, half = chan * blk, blk // 2
    feeds = blk * 8
    per, width = N1 // blk, HALF // chan
    chunks = per
    twiddle, table = tables()
    dma = pltpu.SemaphoreType.DMA
    blocks = [
        pltpu.VMEM((pieces, parts // 2, sets * width * per // pieces, 128), jnp.bfloat16)
        for sets in (1, 2)
        for pieces in (1, chunks)
    ]
    any_place = pl.BlockSpec(memory_space=pl.ANY)
    near = (per, half, width * 12, 2 * feeds)
    far = (per, half, width * 4, 2 * feeds)
    mine = pl.pallas_call(
        functools.partial(exchange_kernel, (frames, chan, blk)),
        out_shape=[jax.ShapeDtypeStruct(near, jnp.bfloat16), jax.ShapeDtypeStruct(far, jnp.bfloat16)],
        in_specs=whole(4),
        out_specs=[any_place, any_place],
        scratch_shapes=[
            pltpu.VMEM((8, (TAPS - 1) * L), jnp.bfloat16),
            pltpu.VMEM((frames * N1, 8, N2), jnp.float32),
            pltpu.VMEM((2 * N1, 4 * frames, 2 * N2), jnp.float32),
            *blocks,
            *blocks,
            pltpu.VMEM((feeds * width, 128), jnp.float32),
            pltpu.VMEM((feeds // 2 * width, 128), jnp.float32),
            pltpu.VMEM(near, jnp.bfloat16),
            pltpu.VMEM(far, jnp.bfloat16),
            dma((2,)),
            dma((2, 1 + chunks)),
            dma((2, 1 + chunks)),
            dma((2, per)),
            dma((2,)),
        ],
        compiler_params=pltpu.CompilerParams(vmem_limit_bytes=VMEM, collective_id=0, has_side_effects=True),
        name="exchange",
    )(voltages, fir_taps, jnp.asarray(twiddle), jnp.asarray(table))
    return pl.pallas_call(
        functools.partial(finish_kernel, blk, per, width, feeds),
        out_shape=jax.ShapeDtypeStruct((2, 8, feeds, width * N1), jnp.float32),
        in_specs=whole(2),
        out_specs=any_place,
        scratch_shapes=[
            pltpu.VMEM((feeds // 64, width * N1 * 8, 128), jnp.float32),
            pltpu.VMEM((8, 2, feeds, width * N1), jnp.float32),
            dma((8, 2)),
        ],
        compiler_params=pltpu.CompilerParams(vmem_limit_bytes=VMEM),
        name="finish",
    )(*mine)


def solution(mesh):
    chan, blk = mesh.shape["chan"], mesh.shape["blk"]
    return jax.shard_map(
        functools.partial(on_device, chan, blk),
        mesh=mesh,
        in_specs=(P("blk", "chan"), P()),
        out_specs=P(None, "blk", None, "chan"),
        check_vma=False,
    )
```
